32 devices in a mesh: dp: 8 (over z, x), mp: 4 (over y, core).
Axes of the slice: x: 2, y: 2, z: 4, core: 2. Of those that a mesh axis runs over, the one named last changes fastest.
Arguments:
- queries: bfloat16 [8, 512, 2048], P('dp', 'mp'), may hold values from -6 to 6
- keys: bfloat16 [8, 512, 1024], P('dp'), may hold values from -6 to 6
- values: bfloat16 [8, 512, 1024], P('dp'), may hold values from -6 to 6
- stream: bfloat16 [8, 512, 3584], P('dp', None, 'mp'), may hold values from -6 to 6
- out_proj: bfloat16 [2048, 3584], P(None, 'mp'), may hold values from -0.125 to 0.125
- norm_gain: float32 [3584], P('mp'), may hold values from 0.1 to 1.9
- tag_proj: bfloat16 [3584, 128], P('mp'), may hold values from -0.03125 to 0.03125
- direction: float32 [2048, 3584], P('dp', 'mp'), may hold values from -120 to 120
- starts: int32 [8, 4], P('dp'), may hold values from 0 to 511, as said below
- tags: int32 [8, 512], P('dp'), may hold values from 0 to 127
Outputs:
- iterate: float32 [2048, 3584], P('dp', 'mp')
The draws below stay inside these ranges and needn't reach their ends.
Inputs may be any that keep to these rules, and one draw needn't show every extreme that they name: `starts`: each sequence's first entry is 0 and the entries rise strictly, so every file holds one token or more.
All inputs are finite; a program needn't handle non-finite values.
Results may differ from the reference program's by a relative error of at most 0.0032.
Values may be sent and summed in bfloat16 or wider, within the bound.
A program may use at most 64 MiB of HBM per device.

```python
import jax
import jax.numpy as jnp
from jax import lax

D = 3584
HD = 256
HQ = 8
HK = 4
TAGS = 128
WINDOW = 256
FILES = 4
ITERS = 2
LEN = 512
SEQS = 8


def draw_direction(key, part):
    key = jax.random.fold_in(key, 11)
    k_base, k_rows, k_cols = jax.random.split(key, 3)
    rows = HQ * HD
    rising = 3.0 ** (jnp.arange(rows, dtype=jnp.float32)[:, None] / rows)
    row_scale = rising * jnp.exp(jax.random.uniform(k_rows, (rows, 1), jnp.float32, 0.0, jnp.log(10.0)))
    col_scale = jnp.exp(jax.random.uniform(k_cols, (1, D), jnp.float32, 0.0, jnp.log(10.0)))
    base = jnp.clip(jax.random.normal(k_base, (rows, D), jnp.float32), -4.0, 4.0)
    return (0.1 * base * row_scale * col_scale).astype(jnp.float32)


def draw_starts(key, part):
    key = jax.random.fold_in(key, 12)
    seq_keys = jax.random.split(key, SEQS)

    def one(seq_key):
        cuts = jax.random.permutation(seq_key, LEN - 1)[:FILES - 1] + 1
        cuts = jnp.sort(cuts.astype(jnp.int32))
        return jnp.concatenate([jnp.zeros((1,), jnp.int32), cuts])
    return jax.vmap(one)(seq_keys).astype(jnp.int32)


def set_ends(values, own_key, low, largest):
    shape = values.shape
    place = [jax.random.randint(jax.random.fold_in(own_key, axis), (), 0, shape[axis]) for axis in range(len(shape))]
    values = values.at[tuple(place)].set(low)
    longest = shape.index(max(shape))
    place[longest] = (place[longest] + 1) % shape[longest]
    return values.at[tuple(place)].set(largest)


def steps_of(stream_key, extent, cuts, low, largest):
    factor_of = 1.0
    for position, shards_of in cuts:
        steps = jax.random.uniform(jax.random.fold_in(jax.random.fold_in(stream_key, 6), position), (shards_of,), jnp.float32, low / len(cuts), largest / len(cuts))
        factor_of = factor_of * jnp.repeat(jnp.exp(steps), extent[position] // shards_of).reshape((-1,) + (1,) * (len(extent) - 1 - position))
    return factor_of


def normal_values(own_key, shape, deviation, bound, pieces=(), kind=jnp.bfloat16):
    loudness = steps_of(own_key, shape, pieces, -0.22, 0.18) if pieces else 1.0
    array = jax.random.normal(own_key, shape, jnp.float32) * deviation * loudness
    return jnp.minimum(jnp.maximum(array, -bound), bound).astype(kind)


def setup_inputs(seed: int = 0) -> dict:
    streams_of = jax.random.split(jax.random.key(seed), 11)
    queries = normal_values(streams_of[0], (SEQS, LEN, HQ * HD), 1.0, 6.0, ((0, 8), (1, 4)))
    keys = normal_values(streams_of[1], (SEQS, LEN, HK * HD), 1.0, 6.0, ((0, 8),))
    values = normal_values(streams_of[2], (SEQS, LEN, HK * HD), 1.0, 6.0, ((0, 8),))
    stream = normal_values(streams_of[3], (SEQS, LEN, D), 1.0, 6.0, ((0, 8), (2, 4)))
    out_proj = normal_values(streams_of[4], (HQ * HD, D), (HQ * HD) ** -0.5, 0.125, ((1, 4),))
    norm_gain = jnp.clip(1.0 + 0.18 * jax.random.normal(streams_of[5], (D,), jnp.float32), 0.1, 1.9)
    tag_proj = normal_values(streams_of[6], (D, TAGS), (8 * D) ** -0.5, 0.03125, ((0, 4),))
    direction = draw_direction(jax.random.fold_in(streams_of[10], 71), 0)
    starts = draw_starts(jax.random.fold_in(streams_of[10], 71), 0)
    tags = set_ends(jax.random.randint(streams_of[9], (SEQS, LEN), 0, TAGS), jax.random.fold_in(streams_of[9], 1), 0, TAGS - 1).astype(jnp.int32)
    return {"queries": queries, "keys": keys, "values": values, "stream": stream, "out_proj": out_proj, "norm_gain": norm_gain, "tag_proj": tag_proj, "direction": direction, "starts": starts, "tags": tags}


DAMP = 0.01
NORM_EPS = 1e-06
MEAN_EPS = 1e-06

def attend(query, key, value, start, offset):
    num_q = query.shape[0]
    num_k = key.shape[0]
    group = HQ // HK
    q_heads = query.reshape(num_q, HK, group, HD)
    k_heads = key.reshape(num_k, HK, HD)
    v_heads = value.reshape(num_k, HK, HD)
    scores = jnp.einsum('qgrd,kgd->grqk', q_heads.astype(jnp.float32), k_heads.astype(jnp.float32)) / jnp.sqrt(jnp.float32(HD))
    scores = 50.0 * jnp.tanh(scores / 50.0)
    q_pos = offset + jnp.arange(num_q, dtype=jnp.int32)
    k_pos = jnp.arange(num_k, dtype=jnp.int32)
    q_file = lax.optimization_barrier(jnp.sum((start[None, :] <= q_pos[:, None]).astype(jnp.int32), 1)) - 1
    k_file = lax.optimization_barrier(jnp.sum((start[None, :] <= k_pos[:, None]).astype(jnp.int32), 1)) - 1
    allowed = (q_file[:, None] == k_file[None, :]) & (k_pos[None, :] <= q_pos[:, None]) & (q_pos[:, None] - k_pos[None, :] < WINDOW)
    expo = jnp.where(allowed[None, None], jnp.exp(scores), 0.0)
    weights = (expo / lax.optimization_barrier(jnp.sum(expo, -1, keepdims=True))).astype(jnp.bfloat16)
    out = jnp.einsum('grqk,kgd->qgrd', weights.astype(jnp.float32), v_heads.astype(jnp.float32))
    return out.reshape(num_q, HQ * HD).astype(jnp.bfloat16)

def reference(queries, keys, values, stream, out_proj, norm_gain, tag_proj, direction, starts, tags):
    attn = lax.map(lambda item: attend(item[0], item[1], item[2], item[3], 0), (queries, keys, values, starts))
    flat = attn.reshape(-1, HQ * HD)
    h_all = stream.astype(jnp.float32).reshape(-1, D) + jnp.dot(flat, out_proj, preferred_element_type=jnp.float32)
    wide = tag_proj.astype(jnp.float32)
    tag_ids = jnp.arange(TAGS, dtype=jnp.int32)

    def token_loss(hh, target):
        sumsq = lax.optimization_barrier(jnp.sum(hh * hh, -1))
        rscale = (sumsq / D + NORM_EPS) ** (-0.5)
        zval = jnp.dot(hh * norm_gain, wide, precision=lax.Precision.HIGHEST)
        logits = 30.0 * jnp.tanh(rscale[:, None] * zval / 30.0)
        total = jnp.log(lax.optimization_barrier(jnp.sum(jnp.exp(logits), -1)))
        picked = lax.optimization_barrier(jnp.sum(jnp.where(target[:, None] == tag_ids[None, :], logits, 0.0), -1))
        return jnp.sum(total - picked)

    def curvature(hdot):

        def one(item):
            hh, hd, target = item
            grad_fn = jax.grad(lambda x: token_loss(x, target))
            return jax.jvp(grad_fn, (hh,), (hd,))[1]
        out = lax.map(one, (h_all.reshape(SEQS, LEN, D), hdot.reshape(SEQS, LEN, D), tags))
        return out.reshape(-1, D).astype(jnp.bfloat16)

    def product(u):
        hdot = jnp.dot(flat, u.astype(jnp.bfloat16), preferred_element_type=jnp.float32)
        gdot = curvature(hdot)
        return lax.dot_general(flat, gdot, (((0,), (0,)), ((), ())), preferred_element_type=jnp.float32)
    count = HQ * HD * D
    u = direction
    sigma = jnp.float32(1.0)
    for step in range(ITERS):
        hvp = product(u)
        if step == 0:
            sigma = 2.0 * jnp.sqrt((jnp.sum(hvp * hvp) / count + MEAN_EPS) / (jnp.sum(direction * direction) / count + MEAN_EPS))
        u = direction + (1.0 - DAMP) * u - hvp / sigma
    return u
```

```python
import functools

import jax
import jax.numpy as jnp
from jax import lax
from jax.experimental import pallas as pl
from jax.experimental.pallas import tpu as pltpu
from jax.sharding import PartitionSpec as P

D = 3584
HD = 256
HQ = 8
HK = 4
TAGS = 128
WINDOW = 256

DAMP = 0.01
NORM_EPS = 1e-06
MEAN_EPS = 1e-06

MESH = pl.DeviceIdType.MESH
VMEM_LIMIT = 48 * 1024 * 1024
CHUNKS = 2
F32 = jnp.float32
BF16 = jnp.bfloat16


def inner_of(size):
    return 1 << ((size.bit_length() - 1) // 2)


def remote(src, dst, send, recv, dp, mp):
    return pltpu.make_async_remote_copy(
        src_ref=src,
        dst_ref=dst,
        send_sem=send,
        recv_sem=recv,
        device_id=(dp, mp),
        device_id_type=MESH,
    )


def greet(peers):
    barrier = pltpu.get_barrier_semaphore()
    for dp, mp in peers:
        pl.semaphore_signal(barrier, inc=1, device_id=(dp, mp), device_id_type=MESH)
    pl.semaphore_wait(barrier, len(peers))


class Grid:
    def __init__(self, size):
        self.size = size
        self.inner = inner_of(size)
        self.outer = size // self.inner
        self.mp = lax.axis_index("mp")
        me = lax.axis_index("dp")
        self.z = me // self.inner
        self.x = me % self.inner

    def at(self, dz, dx):
        z = lax.rem(self.z + (dz + self.outer), self.outer)
        x = lax.rem(self.x + (dx + self.inner), self.inner)
        return z * self.inner + x

    def peers(self):
        out = [(self.at(dz, 0), self.mp) for dz in range(1, self.outer)]
        return out + [(self.at(0, dx), self.mp) for dx in range(1, self.inner)]


def part_rows(ref, device, rows, chunk):
    step = rows // CHUNKS
    return ref.at[pl.ds(pl.multiple_of(device * rows + chunk * step, step), step)]


def gather_start(grid, src, dst, local, send, recv):
    rows = src.shape[0]
    step = rows // CHUNKS
    me = grid.at(0, 0)
    sent = []
    for c in range(CHUNKS):
        piece = src.at[pl.ds(c * step, step)]
        place = part_rows(dst, me, rows, c)
        for dz in range(1, grid.outer):
            sent.append(remote(piece, place, send.at[dz, 0, c], recv.at[dz, 0, c], grid.at(dz, 0), grid.mp))
        for dx in range(1, grid.inner):
            sent.append(remote(piece, place, send.at[0, dx, c], recv.at[0, dx, c], grid.at(0, dx), grid.mp))
    for copy in sent:
        copy.start()
    own = pltpu.make_async_copy(src, dst.at[pl.ds(pl.multiple_of(me * rows, rows), rows)], local)
    own.start()
    return own, sent


def gather_finish(grid, src, dst, started, send, recv):
    rows = src.shape[0]
    own, sent = started
    for c in range(CHUNKS):
        for dz in range(1, grid.outer):
            place = part_rows(dst, grid.at(-dz, 0), rows, c)
            remote(place, place, send.at[dz, 0, c], recv.at[dz, 0, c], grid.at(dz, 0), grid.mp).wait_recv()
            for dx in range(1, grid.inner):
                copy = remote(place, place, send.at[dz, dx, c], recv.at[dz, dx, c], grid.at(0, dx), grid.mp)
                copy.start()
                sent.append(copy)
    for c in range(CHUNKS):
        for dz in range(grid.outer):
            for dx in range(1, grid.inner):
                place = part_rows(dst, grid.at(-dz, -dx), rows, c)
                remote(place, place, send.at[dz, dx, c], recv.at[dz, dx, c], grid.at(0, dx), grid.mp).wait_recv()
    own.wait()
    for copy in sent:
        copy.wait_send()


def first_kernel(size, starts, query, key, value, src, attn, gathered, mine, local, send, recv, send_m, recv_m):
    grid = Grid(size)
    q_rows, width = query.shape
    num_k = key.shape[0]
    ways = num_k // q_rows
    dp = lax.axis_index("dp")
    mp = grid.mp
    others = [lax.rem(mp + d, ways) for d in range(1, ways)]
    greet(grid.peers() + [(dp, other) for other in others])
    started = gather_start(grid, src, gathered, local.at[0], send, recv)

    q_pos = mp * q_rows + lax.broadcasted_iota(jnp.int32, (q_rows, num_k), 0)
    k_pos = lax.broadcasted_iota(jnp.int32, (q_rows, num_k), 1)
    q_file = jnp.zeros((q_rows, num_k), jnp.int32)
    k_file = jnp.zeros((q_rows, num_k), jnp.int32)
    for f in range(starts.shape[1]):
        q_file = q_file + (starts[0, f] <= q_pos).astype(jnp.int32)
        k_file = k_file + (starts[0, f] <= k_pos).astype(jnp.int32)
    allowed = (q_file == k_file) & (k_pos <= q_pos) & (q_pos - k_pos < WINDOW)
    for h in range(HQ):
        g = h // (HQ // HK)
        scores = lax.dot_general(
            query[:, h * HD : (h + 1) * HD],
            key[:, g * HD : (g + 1) * HD],
            (((1,), (1,)), ((), ())),
            preferred_element_type=F32,
        ) * (1.0 / HD**0.5)
        scores = 50.0 * jnp.tanh(scores / 50.0)
        expo = jnp.where(allowed, jnp.exp(scores), 0.0)
        weights = (expo / jnp.sum(expo, -1, keepdims=True)).astype(BF16)
        out = jnp.dot(weights, value[:, g * HD : (g + 1) * HD], preferred_element_type=F32)
        mine[:, h * HD : (h + 1) * HD] = out.astype(BF16)

    def rows_of(device):
        return attn.at[pl.ds(pl.multiple_of(device * q_rows, q_rows), q_rows)]

    sent = [
        remote(mine, rows_of(mp), send_m.at[d], recv_m.at[d], dp, other) for d, other in enumerate(others)
    ]
    for copy in sent:
        copy.start()
    own = pltpu.make_async_copy(mine, rows_of(mp), local.at[1])
    own.start()
    gather_finish(grid, src, gathered, started, send, recv)
    for d, other in enumerate(others):
        place = rows_of(lax.rem(mp + (ways - 1 - d), ways))
        remote(place, place, send_m.at[d], recv_m.at[d], dp, other).wait_recv()
    own.wait()
    for copy in sent:
        copy.wait_send()


def first(size, ways, starts, query, key, value, src):
    rows, cols = src.shape
    inner = inner_of(size)
    sems = pltpu.SemaphoreType.DMA((size // inner, inner, CHUNKS))
    vmem = pl.BlockSpec(memory_space=pltpu.VMEM)
    place = pl.BlockSpec(memory_space=pl.ANY)
    return pl.pallas_call(
        functools.partial(first_kernel, size),
        out_shape=(
            jax.ShapeDtypeStruct((key.shape[0], query.shape[1]), BF16),
            jax.ShapeDtypeStruct((rows * size, cols), BF16),
        ),
        in_specs=[pl.BlockSpec(memory_space=pltpu.SMEM), vmem, vmem, vmem, place],
        out_specs=(place, place),
        scratch_shapes=[
            pltpu.VMEM(query.shape, BF16),
            pltpu.SemaphoreType.DMA((2,)),
            sems,
            sems,
            pltpu.SemaphoreType.DMA((ways,)),
            pltpu.SemaphoreType.DMA((ways,)),
        ],
        compiler_params=pltpu.CompilerParams(
            collective_id=0, has_side_effects=True, vmem_limit_bytes=VMEM_LIMIT
        ),
        name="attend_and_gather",
    )(starts, query, key, value, src)


def curve_kernel(ways, early, *refs):
    if early:
        part, tags, packed, z_out, r_out, extra_out, got, mine, s1, r1, s2, r2 = refs
    else:
        part, tags, z_in, r_in, packed, extra_out, got, mine, s1, r1, s2, r2 = refs
    rows = part.shape[0] // ways
    dp = lax.axis_index("dp")
    mp = lax.axis_index("mp")
    others = [lax.rem(mp + d, ways) for d in range(1, ways)]
    greet([(dp, other) for other in others])

    def rows_of(device):
        return pl.ds(pl.multiple_of(device * rows, rows), rows)

    sent = [
        remote(part.at[rows_of(other)], got.at[d], s1.at[d], r1.at[d], dp, other)
        for d, other in enumerate(others)
    ]
    for copy in sent:
        copy.start()
    total = part[rows_of(mp), :].astype(F32)
    for d, copy in enumerate(sent):
        copy.wait_recv()
        total = total + got[d].astype(F32)
    if early:
        zval = total[:, :TAGS]
        zdot = total[:, TAGS : 2 * TAGS]
        extra = total[:, 2 * TAGS :]
        sumsq = extra[:, 2:3] + extra[:, 3:4]
        rscale = lax.rsqrt(sumsq / D + NORM_EPS)
        z_out[...] = zval
        r_out[...] = jnp.broadcast_to(rscale, r_out.shape)
    else:
        zdot = total[:, :TAGS]
        extra = total[:, TAGS:]
        zval = z_in[...]
        rscale = r_in[:, 0:1]
    along = extra[:, 0:1] + extra[:, 1:2]
    extra_out[...] = extra[:8, :]
    tanh_val = jnp.tanh(rscale * zval / 30.0)
    slope = 1.0 - tanh_val * tanh_val
    expo = jnp.exp(30.0 * tanh_val)
    probs = expo / jnp.sum(expo, -1, keepdims=True)
    lane = lax.broadcasted_iota(jnp.int32, zval.shape, 1)
    onehot = (tags[rows_of(mp), :] == lane).astype(F32)
    dlogit = probs - onehot
    wgrad = dlogit * slope
    rho = jnp.sum(wgrad * zval, -1, keepdims=True)
    cube = rscale * rscale * rscale / D
    rdot = -cube * along
    mdot = rdot * zval + rscale * zdot
    ldot = slope * mdot
    pdot = probs * (ldot - jnp.sum(probs * ldot, -1, keepdims=True))
    wdot = pdot * slope - dlogit * 2.0 * tanh_val * slope * mdot / 30.0
    rhodot = jnp.sum(wdot * zval + wgrad * zdot, -1, keepdims=True)
    mixed = rdot * wgrad + rscale * wdot
    coeff = rhodot * cube + 3.0 * rho * rscale * rscale * rdot / D
    pull = rho * cube
    coeff_high = coeff.astype(BF16).astype(F32)
    pull_high = pull.astype(BF16).astype(F32)
    columns = jnp.where(lane == 0, coeff_high, 0.0)
    columns = jnp.where(lane == 1, coeff - coeff_high, columns)
    columns = jnp.where(lane == 2, pull_high, columns)
    columns = jnp.where(lane == 3, pull - pull_high, columns)
    mine[:, :TAGS] = mixed.astype(BF16)
    mine[:, TAGS:] = columns.astype(BF16)
    back = [
        remote(mine, packed.at[rows_of(mp)], s2.at[d], r2.at[d], dp, other)
        for d, other in enumerate(others)
    ]
    for copy in back:
        copy.start()
    packed[rows_of(mp), :] = mine[...]
    for d, other in enumerate(others):
        place = packed.at[rows_of(lax.rem(mp + (ways - 1 - d), ways))]
        remote(place, place, s2.at[d], r2.at[d], dp, other).wait_recv()
    for copy in sent + back:
        copy.wait_send()


def curve(ways, part, tags, state, collective_id):
    early = state is None
    tokens, width = part.shape
    rows = tokens // ways
    vmem = pl.BlockSpec(memory_space=pltpu.VMEM)
    operands = (part, tags) if early else (part, tags) + state
    out_shape = [jax.ShapeDtypeStruct((tokens, 2 * TAGS), BF16)]
    if early:
        out_shape += [jax.ShapeDtypeStruct((rows, TAGS), F32)] * 2
    out_shape += [jax.ShapeDtypeStruct((8, TAGS), F32)]
    sems = pltpu.SemaphoreType.DMA((ways,))
    return pl.pallas_call(
        functools.partial(curve_kernel, ways, early),
        out_shape=tuple(out_shape),
        in_specs=[vmem] * len(operands),
        out_specs=(vmem,) * len(out_shape),
        scratch_shapes=[
            pltpu.VMEM((ways - 1, rows, width), BF16),
            pltpu.VMEM((rows, 2 * TAGS), BF16),
            sems,
            sems,
            sems,
            sems,
        ],
        compiler_params=pltpu.CompilerParams(
            collective_id=collective_id, has_side_effects=True, vmem_limit_bytes=VMEM_LIMIT
        ),
        name="curve_early" if early else "curve_late",
    )(*operands)


def reduce_rows(grid, src, own, from_x, pair, from_z, send, recv):
    rows = own.shape[0]
    step = rows // CHUNKS
    sent = []

    def piece(ref, c):
        return ref.at[pl.ds(c * step, step)]

    order = list(range(1, grid.outer)) + [0]
    for dz in order:
        for c in range(CHUNKS):
            for dx in range(1, grid.inner):
                copy = remote(
                    part_rows(src, grid.at(dz, dx), rows, c),
                    piece(from_x.at[dz, dx - 1], c),
                    send.at[dz, dx, c],
                    recv.at[dz, dx, c],
                    grid.at(0, dx),
                    grid.mp,
                )
                copy.start()
                sent.append(copy)

    def paired(dz, c):
        total = part_rows(src, grid.at(dz, 0), rows, c)[...].astype(F32)
        for dx in range(1, grid.inner):
            place = piece(from_x.at[dz, dx - 1], c)
            remote(place, place, send.at[dz, dx, c], recv.at[dz, dx, c], grid.at(0, dx), grid.mp).wait_recv()
            total = total + place[...].astype(F32)
        return total

    for dz in range(1, grid.outer):
        for c in range(CHUNKS):
            place = piece(pair.at[dz - 1], c)
            place[...] = paired(dz, c).astype(BF16)
            copy = remote(
                place,
                piece(from_z.at[dz - 1], c),
                send.at[dz, 0, c],
                recv.at[dz, 0, c],
                grid.at(dz, 0),
                grid.mp,
            )
            copy.start()
            sent.append(copy)
    for c in range(CHUNKS):
        total = paired(0, c)
        for dz in range(1, grid.outer):
            place = piece(from_z.at[dz - 1], c)
            remote(place, place, send.at[dz, 0, c], recv.at[dz, 0, c], grid.at(dz, 0), grid.mp).wait_recv()
            total = total + place[...].astype(F32)
        piece(own, c)[...] = total
    return sent


def reduce_scratch(size, rows, cols):
    inner = inner_of(size)
    outer = size // inner
    sems = pltpu.SemaphoreType.DMA((outer, inner, CHUNKS))
    return [
        pltpu.VMEM((outer, inner - 1, rows, cols), BF16),
        pltpu.VMEM((outer - 1, rows, cols), BF16),
        pltpu.VMEM((outer - 1, rows, cols), BF16),
        sems,
        sems,
    ]


def sum_gather_kernel(size, src, own, gathered, from_x, pair, from_z, s1, r1, mine, local, s2, r2):
    grid = Grid(size)
    greet(grid.peers())
    sent = reduce_rows(grid, src, own, from_x, pair, from_z, s1, r1)
    mine[...] = own[...].astype(BF16)
    started = gather_start(grid, mine, gathered, local.at[0], s2, r2)
    gather_finish(grid, mine, gathered, started, s2, r2)
    for copy in sent:
        copy.wait_send()


def sum_gather(size, src):
    total, cols = src.shape
    rows = total // size
    inner = inner_of(size)
    sems = pltpu.SemaphoreType.DMA((size // inner, inner, CHUNKS))
    vmem = pl.BlockSpec(memory_space=pltpu.VMEM)
    return pl.pallas_call(
        functools.partial(sum_gather_kernel, size),
        out_shape=(
            jax.ShapeDtypeStruct((rows, cols), F32),
            jax.ShapeDtypeStruct((total, cols), BF16),
        ),
        in_specs=[vmem],
        out_specs=(vmem, pl.BlockSpec(memory_space=pl.ANY)),
        scratch_shapes=reduce_scratch(size, rows, cols)
        + [pltpu.VMEM((rows, cols), BF16), pltpu.SemaphoreType.DMA((1,)), sems, sems],
        compiler_params=pltpu.CompilerParams(
            collective_id=2, has_side_effects=True, vmem_limit_bytes=VMEM_LIMIT
        ),
        name="sum_and_gather",
    )(src)


def sum_kernel(size, src, scalars, own, scalar_sum, from_x, pair, from_z, s1, r1, got, s2, r2):
    grid = Grid(size)
    others = [lax.rem(lax.axis_index("dp") + d, size) for d in range(1, size)]
    greet([(other, grid.mp) for other in others])
    small = [
        remote(scalars, got.at[d], s2.at[d], r2.at[d], other, grid.mp) for d, other in enumerate(others)
    ]
    for copy in small:
        copy.start()
    sent = reduce_rows(grid, src, own, from_x, pair, from_z, s1, r1)
    total = scalars[...]
    for d, copy in enumerate(small):
        copy.wait_recv()
        total = total + got[d]
    scalar_sum[...] = total
    for copy in sent + small:
        copy.wait_send()


def sum_only(size, src, scalars):
    total, cols = src.shape
    rows = total // size
    vmem = pl.BlockSpec(memory_space=pltpu.VMEM)
    return pl.pallas_call(
        functools.partial(sum_kernel, size),
        out_shape=(
            jax.ShapeDtypeStruct((rows, cols), F32),
            jax.ShapeDtypeStruct(scalars.shape, F32),
        ),
        in_specs=[vmem, vmem],
        out_specs=(vmem, vmem),
        scratch_shapes=reduce_scratch(size, rows, cols)
        + [
            pltpu.VMEM((size - 1,) + scalars.shape, F32),
            pltpu.SemaphoreType.DMA((size - 1,)),
            pltpu.SemaphoreType.DMA((size - 1,)),
        ],
        compiler_params=pltpu.CompilerParams(
            collective_id=4, has_side_effects=True, vmem_limit_bytes=VMEM_LIMIT
        ),
        name="sum_rows",
    )(src, scalars)


def split_columns(values, tokens):
    out = []
    for value in values:
        value = jnp.broadcast_to(value, (tokens,))
        high = lax.reduce_precision(value, 8, 7)
        out += [high, value - high]
    block = jnp.stack(out, -1).astype(BF16)
    return jnp.pad(block, ((0, 0), (0, TAGS - len(out))))


def local(size, ways, queries, keys, values, stream, out_proj, norm_gain, tag_proj, direction, starts, tags):
    count = HQ * HD * D
    tokens = keys.shape[1]
    tag_column = tags[0][:, None]
    attn, rounded = first(
        size, ways, starts, queries[0], keys[0], values[0], direction.astype(BF16)
    )
    h_loc = stream[0].astype(F32) + jnp.dot(attn, out_proj, preferred_element_type=F32)

    def scores(value):
        return jnp.dot((value * norm_gain).astype(BF16), tag_proj, preferred_element_type=F32).astype(BF16)

    def product(packed, hdot):
        mixed = packed[:, :TAGS]
        columns = packed[:, TAGS : TAGS + 4].astype(F32)
        coeff = columns[:, 0:1] + columns[:, 1:2]
        pull = columns[:, 2:3] + columns[:, 3:4]
        back = lax.dot_general(mixed, tag_proj, (((1,), (1,)), ((), ())), preferred_element_type=F32)
        gdot = (back * norm_gain - coeff * h_loc - pull * hdot).astype(BF16)
        return lax.dot_general(attn, gdot, (((0,), (0,)), ((), ())), preferred_element_type=F32).astype(BF16)

    hdot = jnp.dot(attn, rounded, preferred_element_type=F32)
    extra = split_columns([jnp.sum(h_loc * hdot, -1), jnp.sum(h_loc * h_loc, -1)], tokens)
    part = jnp.concatenate([scores(h_loc), scores(hdot), extra], 1)
    packed, zval, rscale, _ = curve(ways, part, tag_column, None, 1)
    once, once_all = sum_gather(size, product(packed, hdot))

    hdot = jnp.dot(attn, once_all, preferred_element_type=F32)
    extra = split_columns(
        [jnp.sum(h_loc * hdot, -1), jnp.sum(direction * direction), jnp.sum(once * once)], tokens
    )
    part = jnp.concatenate([scores(hdot), extra], 1)
    packed, scalars = curve(ways, part, tag_column, (zval, rscale), 3)
    twice, sums = sum_only(size, product(packed, hdot), scalars)

    early_norm = sums[0, 2] + sums[0, 3]
    product_sq = sums[0, 4] + sums[0, 5]
    sigma = 2.0 * jnp.sqrt((product_sq / count + MEAN_EPS) / (early_norm / count + MEAN_EPS))
    keep = 1.0 - DAMP
    return (
        (1.0 + keep * (1.0 + keep)) * direction
        - ((1.0 + 2.0 * keep) / sigma) * once
        + twice / sigma / sigma
    )


def solution(mesh):
    return jax.shard_map(
        functools.partial(local, mesh.shape["dp"], mesh.shape["mp"]),
        mesh=mesh,
        in_specs=(
            P("dp", "mp", None),
            P("dp", None, None),
            P("dp", None, None),
            P("dp", None, "mp"),
            P(None, "mp"),
            P("mp"),
            P("mp", None),
            P("dp", "mp"),
            P("dp", None),
            P("dp", None),
        ),
        out_specs=P("dp", "mp"),
        check_vma=False,
    )
```

```python
import functools

import jax
import jax.numpy as jnp
from jax import lax
from jax.experimental import pallas as pl
from jax.experimental.pallas import tpu as pltpu
from jax.sharding import PartitionSpec as P

D = 3584
HD = 256
HQ = 8
HK = 4
TAGS = 128
WINDOW = 256

DAMP = 0.01
NORM_EPS = 1e-06
MEAN_EPS = 1e-06

MESH = pl.DeviceIdType.MESH
VMEM_LIMIT = 48 * 1024 * 1024
CHUNKS = 2
AHEAD = 2
F32 = jnp.float32
BF16 = jnp.bfloat16


def inner_of(size):
    return 1 << ((size.bit_length() - 1) // 2)


def remote(src, dst, send, recv, dp, mp):
    return pltpu.make_async_remote_copy(
        src_ref=src,
        dst_ref=dst,
        send_sem=send,
        recv_sem=recv,
        device_id=(dp, mp),
        device_id_type=MESH,
    )


def greet(peers):
    barrier = pltpu.get_barrier_semaphore()
    for dp, mp in peers:
        pl.semaphore_signal(barrier, inc=1, device_id=(dp, mp), device_id_type=MESH)
    pl.semaphore_wait(barrier, len(peers))


class Grid:
    def __init__(self, size):
        self.size = size
        self.inner = inner_of(size)
        self.outer = size // self.inner
        self.mp = lax.axis_index("mp")
        me = lax.axis_index("dp")
        self.z = me // self.inner
        self.x = me % self.inner

    def at(self, dz, dx):
        z = lax.rem(self.z + (dz + self.outer), self.outer)
        x = lax.rem(self.x + (dx + self.inner), self.inner)
        return z * self.inner + x

    def peers(self):
        out = [(self.at(dz, 0), self.mp) for dz in range(1, self.outer)]
        return out + [(self.at(0, dx), self.mp) for dx in range(1, self.inner)]


def part_rows(ref, device, rows, chunk):
    step = rows // CHUNKS
    return ref.at[pl.ds(pl.multiple_of(device * rows + chunk * step, step), step)]


class Gather:
    def __init__(self, grid, src, dst, local, send, recv, send_x, recv_x):
        self.grid = grid
        self.src = src
        self.dst = dst
        self.local = local
        self.line = (send, recv)
        self.side = (send_x, recv_x)
        self.rows = src.shape[0]

    def block(self, way, hops, dx, c):
        z = self.grid.z - hops * way
        x = lax.rem(self.grid.x + (dx + self.grid.inner), self.grid.inner)
        return part_rows(self.dst, z * self.grid.inner + x, self.rows, c)

    def arrives(self, way, hops):
        return self.grid.z >= hops if way > 0 else self.grid.z + hops < self.grid.outer

    def goes_on(self, way):
        return self.grid.z < self.grid.outer - 1 if way > 0 else self.grid.z > 0

    def hop(self, piece, way, hops, c):
        send, recv = self.line
        lane = (way + 1) // 2
        dp = (self.grid.z + way) * self.grid.inner + self.grid.x
        return remote(
            piece, self.block(way, hops, 0, c), send.at[lane, hops, c], recv.at[lane, hops + 1, c], dp, self.grid.mp
        )

    def aside(self, piece, way, hops, dx, c):
        send, recv = self.side
        lane = (way + 1) // 2
        return remote(
            piece,
            self.block(way, hops, 0, c),
            send.at[lane, hops, dx, c],
            recv.at[lane, hops, dx, c],
            self.grid.at(0, dx),
            self.grid.mp,
        )

    def own(self, c):
        step = self.rows // CHUNKS
        return self.src.at[pl.ds(c * step, step)]

    def start(self):
        for c in range(CHUNKS):
            for way in (1, -1):
                pl.when(self.goes_on(way))(lambda way=way, c=c: self.hop(self.own(c), way, 0, c).start())
            for dx in range(1, self.grid.inner):
                self.aside(self.own(c), 1, 0, dx, c).start()
        me = self.grid.at(0, 0)
        whole = self.dst.at[pl.ds(pl.multiple_of(me * self.rows, self.rows), self.rows)]
        self.kept = pltpu.make_async_copy(self.src, whole, self.local)
        self.kept.start()

    def take(self, way, hops, c):
        piece = self.block(way, hops, 0, c)
        lane = (way + 1) // 2
        send, recv = self.line
        dp = (self.grid.z - way) * self.grid.inner + self.grid.x
        remote(piece, piece, send.at[lane, hops, c], recv.at[lane, hops, c], dp, self.grid.mp).wait_recv()
        if hops < self.grid.outer - 1:
            pl.when(self.goes_on(way))(lambda: self.hop(piece, way, hops, c).start())
        for dx in range(1, self.grid.inner):
            self.aside(piece, way, hops, dx, c).start()

    def take_aside(self, way, hops, c):
        for dx in range(1, self.grid.inner):
            piece = self.block(way, hops, -dx, c)
            self.aside(piece, way, hops, dx, c).wait_recv()

    def settle(self, way, hops, c):
        piece = self.own(c) if hops == 0 else self.block(way, hops, 0, c)
        if hops < self.grid.outer - 1:
            pl.when(self.goes_on(way))(lambda: self.hop(piece, way, hops, c).wait_send())
        if hops or way > 0:
            for dx in range(1, self.grid.inner):
                self.aside(piece, way, hops, dx, c).wait_send()

    def finish(self):
        outer = self.grid.outer
        for act in (self.take, self.take_aside, self.settle):
            for hops in range(outer):
                if hops == 0 and act == self.take:
                    continue
                for c in range(CHUNKS):
                    for way in (1, -1):
                        if hops == 0:
                            if act == self.settle or way > 0:
                                act(way, hops, c)
                        else:
                            pl.when(self.arrives(way, hops))(
                                lambda act=act, way=way, hops=hops, c=c: act(way, hops, c)
                            )
        self.kept.wait()


def gather_scratch(size):
    inner = inner_of(size)
    outer = size // inner
    line = pltpu.SemaphoreType.DMA((2, outer, CHUNKS))
    side = pltpu.SemaphoreType.DMA((2, outer, inner, CHUNKS))
    return [line, line, side, side]


def first_kernel(size, starts, query, key, value, src, attn, gathered, mine, local, send_m, recv_m, *sems):
    grid = Grid(size)
    q_rows, width = query.shape
    num_k = key.shape[0]
    ways = num_k // q_rows
    dp = lax.axis_index("dp")
    mp = grid.mp
    others = [lax.rem(mp + d, ways) for d in range(1, ways)]
    greet(grid.peers() + [(dp, other) for other in others])
    gather = Gather(grid, src, gathered, local.at[0], *sems)
    gather.start()

    q_pos = mp * q_rows + lax.broadcasted_iota(jnp.int32, (q_rows, num_k), 0)
    k_pos = lax.broadcasted_iota(jnp.int32, (q_rows, num_k), 1)
    q_file = jnp.zeros((q_rows, num_k), jnp.int32)
    k_file = jnp.zeros((q_rows, num_k), jnp.int32)
    for f in range(starts.shape[1]):
        q_file = q_file + (starts[0, f] <= q_pos).astype(jnp.int32)
        k_file = k_file + (starts[0, f] <= k_pos).astype(jnp.int32)
    allowed = (q_file == k_file) & (k_pos <= q_pos) & (q_pos - k_pos < WINDOW)
    for h in range(HQ):
        g = h // (HQ // HK)
        scores = lax.dot_general(
            query[:, h * HD : (h + 1) * HD],
            key[:, g * HD : (g + 1) * HD],
            (((1,), (1,)), ((), ())),
            preferred_element_type=F32,
        ) * (1.0 / HD**0.5)
        scores = 50.0 * jnp.tanh(scores / 50.0)
        expo = jnp.where(allowed, jnp.exp(scores), 0.0)
        weights = (expo / jnp.sum(expo, -1, keepdims=True)).astype(BF16)
        out = jnp.dot(weights, value[:, g * HD : (g + 1) * HD], preferred_element_type=F32)
        mine[:, h * HD : (h + 1) * HD] = out.astype(BF16)

    def rows_of(device):
        return attn.at[pl.ds(pl.multiple_of(device * q_rows, q_rows), q_rows)]

    sent = [
        remote(mine, rows_of(mp), send_m.at[d], recv_m.at[d], dp, other) for d, other in enumerate(others)
    ]
    for copy in sent:
        copy.start()
    own = pltpu.make_async_copy(mine, rows_of(mp), local.at[1])
    own.start()
    gather.finish()
    for d, other in enumerate(others):
        place = rows_of(lax.rem(mp + (ways - 1 - d), ways))
        remote(place, place, send_m.at[d], recv_m.at[d], dp, other).wait_recv()
    own.wait()
    for copy in sent:
        copy.wait_send()


def first(size, ways, starts, query, key, value, src):
    rows, cols = src.shape
    vmem = pl.BlockSpec(memory_space=pltpu.VMEM)
    place = pl.BlockSpec(memory_space=pl.ANY)
    return pl.pallas_call(
        functools.partial(first_kernel, size),
        out_shape=(
            jax.ShapeDtypeStruct((key.shape[0], query.shape[1]), BF16),
            jax.ShapeDtypeStruct((rows * size, cols), BF16),
        ),
        in_specs=[pl.BlockSpec(memory_space=pltpu.SMEM), vmem, vmem, vmem, place],
        out_specs=(place, place),
        scratch_shapes=[
            pltpu.VMEM(query.shape, BF16),
            pltpu.SemaphoreType.DMA((2,)),
            pltpu.SemaphoreType.DMA((ways,)),
            pltpu.SemaphoreType.DMA((ways,)),
        ]
        + gather_scratch(size),
        compiler_params=pltpu.CompilerParams(
            collective_id=0, has_side_effects=True, vmem_limit_bytes=VMEM_LIMIT
        ),
        name="attend_and_gather",
    )(starts, query, key, value, src)


def curve_kernel(ways, early, *refs):
    if early:
        part, tags, packed, z_out, r_out, extra_out, got, mine, s1, r1, s2, r2 = refs
    else:
        part, tags, z_in, r_in, packed, extra_out, got, mine, s1, r1, s2, r2 = refs
    rows = part.shape[0] // ways
    dp = lax.axis_index("dp")
    mp = lax.axis_index("mp")
    others = [lax.rem(mp + d, ways) for d in range(1, ways)]
    greet([(dp, other) for other in others])

    def rows_of(device):
        return pl.ds(pl.multiple_of(device * rows, rows), rows)

    sent = [
        remote(part.at[rows_of(other)], got.at[d], s1.at[d], r1.at[d], dp, other)
        for d, other in enumerate(others)
    ]
    for copy in sent:
        copy.start()
    total = part[rows_of(mp), :].astype(F32)
    for d, copy in enumerate(sent):
        copy.wait_recv()
        total = total + got[d].astype(F32)
    if early:
        zval = total[:, :TAGS]
        zdot = total[:, TAGS : 2 * TAGS]
        extra = total[:, 2 * TAGS :]
        sumsq = extra[:, 2:3] + extra[:, 3:4]
        rscale = lax.rsqrt(sumsq / D + NORM_EPS)
        z_out[...] = zval
        r_out[...] = jnp.broadcast_to(rscale, r_out.shape)
    else:
        zdot = total[:, :TAGS]
        extra = total[:, TAGS:]
        zval = z_in[...]
        rscale = r_in[:, 0:1]
    along = extra[:, 0:1] + extra[:, 1:2]
    extra_out[...] = extra[:8, :]
    tanh_val = jnp.tanh(rscale * zval / 30.0)
    slope = 1.0 - tanh_val * tanh_val
    expo = jnp.exp(30.0 * tanh_val)
    probs = expo / jnp.sum(expo, -1, keepdims=True)
    lane = lax.broadcasted_iota(jnp.int32, zval.shape, 1)
    onehot = (tags[rows_of(mp), :] == lane).astype(F32)
    dlogit = probs - onehot
    wgrad = dlogit * slope
    rho = jnp.sum(wgrad * zval, -1, keepdims=True)
    cube = rscale * rscale * rscale / D
    rdot = -cube * along
    mdot = rdot * zval + rscale * zdot
    ldot = slope * mdot
    pdot = probs * (ldot - jnp.sum(probs * ldot, -1, keepdims=True))
    wdot = pdot * slope - dlogit * 2.0 * tanh_val * slope * mdot / 30.0
    rhodot = jnp.sum(wdot * zval + wgrad * zdot, -1, keepdims=True)
    mixed = rdot * wgrad + rscale * wdot
    coeff = rhodot * cube + 3.0 * rho * rscale * rscale * rdot / D
    pull = rho * cube
    coeff_high = coeff.astype(BF16).astype(F32)
    pull_high = pull.astype(BF16).astype(F32)
    columns = jnp.where(lane == 0, coeff_high, 0.0)
    columns = jnp.where(lane == 1, coeff - coeff_high, columns)
    columns = jnp.where(lane == 2, pull_high, columns)
    columns = jnp.where(lane == 3, pull - pull_high, columns)
    mine[:, :TAGS] = mixed.astype(BF16)
    mine[:, TAGS:] = columns.astype(BF16)
    back = [
        remote(mine, packed.at[rows_of(mp)], s2.at[d], r2.at[d], dp, other)
        for d, other in enumerate(others)
    ]
    for copy in back:
        copy.start()
    packed[rows_of(mp), :] = mine[...]
    for d, other in enumerate(others):
        place = packed.at[rows_of(lax.rem(mp + (ways - 1 - d), ways))]
        remote(place, place, s2.at[d], r2.at[d], dp, other).wait_recv()
    for copy in sent + back:
        copy.wait_send()


def curve(ways, part, tags, state, collective_id):
    early = state is None
    tokens, width = part.shape
    rows = tokens // ways
    vmem = pl.BlockSpec(memory_space=pltpu.VMEM)
    operands = (part, tags) if early else (part, tags) + state
    out_shape = [jax.ShapeDtypeStruct((tokens, 2 * TAGS), BF16)]
    if early:
        out_shape += [jax.ShapeDtypeStruct((rows, TAGS), F32)] * 2
    out_shape += [jax.ShapeDtypeStruct((8, TAGS), F32)]
    sems = pltpu.SemaphoreType.DMA((ways,))
    return pl.pallas_call(
        functools.partial(curve_kernel, ways, early),
        out_shape=tuple(out_shape),
        in_specs=[vmem] * len(operands),
        out_specs=(vmem,) * len(out_shape),
        scratch_shapes=[
            pltpu.VMEM((ways - 1, rows, width), BF16),
            pltpu.VMEM((rows, 2 * TAGS), BF16),
            sems,
            sems,
            sems,
            sems,
        ],
        compiler_params=pltpu.CompilerParams(
            collective_id=collective_id, has_side_effects=True, vmem_limit_bytes=VMEM_LIMIT
        ),
        name="curve_early" if early else "curve_late",
    )(*operands)


def reduce_rows(grid, src, own, from_x, pair, from_z, send, recv):
    rows = own.shape[0]
    step = rows // CHUNKS
    sent = []

    def piece(ref, c):
        return ref.at[pl.ds(c * step, step)]

    order = [(dz, c) for dz in list(range(1, grid.outer)) + [0] for c in range(CHUNKS)]
    queue = list(order)

    def feed():
        if queue:
            dz, c = queue.pop(0)
            for dx in range(1, grid.inner):
                copy = remote(
                    part_rows(src, grid.at(dz, dx), rows, c),
                    piece(from_x.at[dz, dx - 1], c),
                    send.at[dz, dx, c],
                    recv.at[dz, dx, c],
                    grid.at(0, dx),
                    grid.mp,
                )
                copy.start()
                sent.append(copy)

    for _ in range(AHEAD):
        feed()

    def paired(dz, c):
        total = part_rows(src, grid.at(dz, 0), rows, c)[...].astype(F32)
        for dx in range(1, grid.inner):
            place = piece(from_x.at[dz, dx - 1], c)
            remote(place, place, send.at[dz, dx, c], recv.at[dz, dx, c], grid.at(0, dx), grid.mp).wait_recv()
            if dx == grid.inner - 1:
                feed()
            total = total + place[...].astype(F32)
        return total

    for dz, c in order:
        if dz == 0:
            continue
        place = piece(pair.at[dz - 1], c)
        place[...] = paired(dz, c).astype(BF16)
        copy = remote(
            place,
            piece(from_z.at[dz - 1], c),
            send.at[dz, 0, c],
            recv.at[dz, 0, c],
            grid.at(dz, 0),
            grid.mp,
        )
        copy.start()
        sent.append(copy)
    for c in range(CHUNKS):
        total = paired(0, c)
        for dz in range(1, grid.outer):
            place = piece(from_z.at[dz - 1], c)
            remote(place, place, send.at[dz, 0, c], recv.at[dz, 0, c], grid.at(dz, 0), grid.mp).wait_recv()
            total = total + place[...].astype(F32)
        piece(own, c)[...] = total
    return sent


def reduce_scratch(size, rows, cols):
    inner = inner_of(size)
    outer = size // inner
    sems = pltpu.SemaphoreType.DMA((outer, inner, CHUNKS))
    return [
        pltpu.VMEM((outer, inner - 1, rows, cols), BF16),
        pltpu.VMEM((outer - 1, rows, cols), BF16),
        pltpu.VMEM((outer - 1, rows, cols), BF16),
        sems,
        sems,
    ]


def sum_gather_kernel(size, src, own, gathered, from_x, pair, from_z, s1, r1, mine, local, *sems):
    grid = Grid(size)
    greet(grid.peers())
    sent = reduce_rows(grid, src, own, from_x, pair, from_z, s1, r1)
    mine[...] = own[...].astype(BF16)
    gather = Gather(grid, mine, gathered, local.at[0], *sems)
    gather.start()
    gather.finish()
    for copy in sent:
        copy.wait_send()


def sum_gather(size, src):
    total, cols = src.shape
    rows = total // size
    vmem = pl.BlockSpec(memory_space=pltpu.VMEM)
    return pl.pallas_call(
        functools.partial(sum_gather_kernel, size),
        out_shape=(
            jax.ShapeDtypeStruct((rows, cols), F32),
            jax.ShapeDtypeStruct((total, cols), BF16),
        ),
        in_specs=[vmem],
        out_specs=(vmem, pl.BlockSpec(memory_space=pl.ANY)),
        scratch_shapes=reduce_scratch(size, rows, cols)
        + [pltpu.VMEM((rows, cols), BF16), pltpu.SemaphoreType.DMA((1,))]
        + gather_scratch(size),
        compiler_params=pltpu.CompilerParams(
            collective_id=2, has_side_effects=True, vmem_limit_bytes=VMEM_LIMIT
        ),
        name="sum_and_gather",
    )(src)


def sum_kernel(size, src, scalars, own, scalar_sum, from_x, pair, from_z, s1, r1, got, s2, r2):
    grid = Grid(size)
    others = [lax.rem(lax.axis_index("dp") + d, size) for d in range(1, size)]
    greet([(other, grid.mp) for other in others])
    small = [
        remote(scalars, got.at[d], s2.at[d], r2.at[d], other, grid.mp) for d, other in enumerate(others)
    ]
    for copy in small:
        copy.start()
    sent = reduce_rows(grid, src, own, from_x, pair, from_z, s1, r1)
    total = scalars[...]
    for d, copy in enumerate(small):
        copy.wait_recv()
        total = total + got[d]
    scalar_sum[...] = total
    for copy in sent + small:
        copy.wait_send()


def sum_only(size, src, scalars):
    total, cols = src.shape
    rows = total // size
    vmem = pl.BlockSpec(memory_space=pltpu.VMEM)
    return pl.pallas_call(
        functools.partial(sum_kernel, size),
        out_shape=(
            jax.ShapeDtypeStruct((rows, cols), F32),
            jax.ShapeDtypeStruct(scalars.shape, F32),
        ),
        in_specs=[vmem, vmem],
        out_specs=(vmem, vmem),
        scratch_shapes=reduce_scratch(size, rows, cols)
        + [
            pltpu.VMEM((size - 1,) + scalars.shape, F32),
            pltpu.SemaphoreType.DMA((size - 1,)),
            pltpu.SemaphoreType.DMA((size - 1,)),
        ],
        compiler_params=pltpu.CompilerParams(
            collective_id=4, has_side_effects=True, vmem_limit_bytes=VMEM_LIMIT
        ),
        name="sum_rows",
    )(src, scalars)


def split_columns(values, tokens):
    out = []
    for value in values:
        value = jnp.broadcast_to(value, (tokens,))
        high = lax.reduce_precision(value, 8, 7)
        out += [high, value - high]
    block = jnp.stack(out, -1).astype(BF16)
    return jnp.pad(block, ((0, 0), (0, TAGS - len(out))))


def local(size, ways, queries, keys, values, stream, out_proj, norm_gain, tag_proj, direction, starts, tags):
    count = HQ * HD * D
    tokens = keys.shape[1]
    tag_column = tags[0][:, None]
    attn, rounded = first(
        size, ways, starts, queries[0], keys[0], values[0], direction.astype(BF16)
    )
    h_loc = stream[0].astype(F32) + jnp.dot(attn, out_proj, preferred_element_type=F32)

    def scores(value):
        return jnp.dot((value * norm_gain).astype(BF16), tag_proj, preferred_element_type=F32).astype(BF16)

    def product(packed, hdot):
        mixed = packed[:, :TAGS]
        columns = packed[:, TAGS : TAGS + 4].astype(F32)
        coeff = columns[:, 0:1] + columns[:, 1:2]
        pull = columns[:, 2:3] + columns[:, 3:4]
        back = lax.dot_general(mixed, tag_proj, (((1,), (1,)), ((), ())), preferred_element_type=F32)
        gdot = (back * norm_gain - coeff * h_loc - pull * hdot).astype(BF16)
        return lax.dot_general(attn, gdot, (((0,), (0,)), ((), ())), preferred_element_type=F32).astype(BF16)

    hdot = jnp.dot(attn, rounded, preferred_element_type=F32)
    extra = split_columns([jnp.sum(h_loc * hdot, -1), jnp.sum(h_loc * h_loc, -1)], tokens)
    part = jnp.concatenate([scores(h_loc), scores(hdot), extra], 1)
    packed, zval, rscale, _ = curve(ways, part, tag_column, None, 1)
    once, once_all = sum_gather(size, product(packed, hdot))

    hdot = jnp.dot(attn, once_all, preferred_element_type=F32)
    extra = split_columns(
        [jnp.sum(h_loc * hdot, -1), jnp.sum(direction * direction), jnp.sum(once * once)], tokens
    )
    part = jnp.concatenate([scores(hdot), extra], 1)
    packed, scalars = curve(ways, part, tag_column, (zval, rscale), 3)
    twice, sums = sum_only(size, product(packed, hdot), scalars)

    early_norm = sums[0, 2] + sums[0, 3]
    product_sq = sums[0, 4] + sums[0, 5]
    sigma = 2.0 * jnp.sqrt((product_sq / count + MEAN_EPS) / (early_norm / count + MEAN_EPS))
    keep = 1.0 - DAMP
    return (
        (1.0 + keep * (1.0 + keep)) * direction
        - ((1.0 + 2.0 * keep) / sigma) * once
        + twice / sigma / sigma
    )


def solution(mesh):
    return jax.shard_map(
        functools.partial(local, mesh.shape["dp"], mesh.shape["mp"]),
        mesh=mesh,
        in_specs=(
            P("dp", "mp", None),
            P("dp", None, None),
            P("dp", None, None),
            P("dp", None, "mp"),
            P(None, "mp"),
            P("mp"),
            P("mp", None),
            P("dp", "mp"),
            P("dp", None),
            P("dp", None),
        ),
        out_specs=P("dp", "mp"),
        check_vma=False,
    )
```

```python
import functools

import jax
import jax.numpy as jnp
from jax import lax
from jax.experimental import pallas as pl
from jax.experimental.pallas import tpu as pltpu
from jax.sharding import PartitionSpec as P

D = 3584
HD = 256
HQ = 8
HK = 4
TAGS = 128
WINDOW = 256

DAMP = 0.01
NORM_EPS = 1e-06
MEAN_EPS = 1e-06

MESH = pl.DeviceIdType.MESH
VMEM_LIMIT = 48 * 1024 * 1024
CHUNKS = 2
STEPS = 4
LANES = 128
F32 = jnp.float32
BF16 = jnp.bfloat16


def inner_of(size):
    return 1 << ((size.bit_length() - 1) // 2)


def remote(src, dst, send, recv, dp, mp):
    return pltpu.make_async_remote_copy(
        src_ref=src,
        dst_ref=dst,
        send_sem=send,
        recv_sem=recv,
        device_id=(dp, mp),
        device_id_type=MESH,
    )


def greet(peers):
    barrier = pltpu.get_barrier_semaphore()
    for dp, mp in peers:
        pl.semaphore_signal(barrier, inc=1, device_id=(dp, mp), device_id_type=MESH)
    pl.semaphore_wait(barrier, len(peers))


class Grid:
    def __init__(self, size):
        self.size = size
        self.inner = inner_of(size)
        self.outer = size // self.inner
        self.mp = lax.axis_index("mp")
        me = lax.axis_index("dp")
        self.z = me // self.inner
        self.x = me % self.inner

    def at(self, dz, dx):
        z = lax.rem(self.z + (dz + self.outer), self.outer)
        x = lax.rem(self.x + (dx + self.inner), self.inner)
        return z * self.inner + x

    def peers(self):
        out = [(self.at(dz, 0), self.mp) for dz in range(1, self.outer)]
        return out + [(self.at(0, dx), self.mp) for dx in range(1, self.inner)]


def part_rows(ref, device, rows, chunk):
    step = rows // CHUNKS
    return ref.at[pl.ds(pl.multiple_of(device * rows + chunk * step, step), step)]


class Gather:
    def __init__(self, grid, src, dst, local, send, recv, send_x, recv_x):
        self.grid = grid
        self.src = src
        self.dst = dst
        self.local = local
        self.line = (send, recv)
        self.side = (send_x, recv_x)
        self.rows = src.shape[0]

    def block(self, way, hops, dx, c):
        z = self.grid.z - hops * way
        x = lax.rem(self.grid.x + (dx + self.grid.inner), self.grid.inner)
        return part_rows(self.dst, z * self.grid.inner + x, self.rows, c)

    def arrives(self, way, hops):
        return self.grid.z >= hops if way > 0 else self.grid.z + hops < self.grid.outer

    def goes_on(self, way):
        return self.grid.z < self.grid.outer - 1 if way > 0 else self.grid.z > 0

    def hop(self, piece, way, hops, c):
        send, recv = self.line
        lane = (way + 1) // 2
        dp = (self.grid.z + way) * self.grid.inner + self.grid.x
        return remote(
            piece, self.block(way, hops, 0, c), send.at[lane, hops, c], recv.at[lane, hops + 1, c], dp, self.grid.mp
        )

    def aside(self, piece, way, hops, dx, c):
        send, recv = self.side
        lane = (way + 1) // 2
        return remote(
            piece,
            self.block(way, hops, 0, c),
            send.at[lane, hops, dx, c],
            recv.at[lane, hops, dx, c],
            self.grid.at(0, dx),
            self.grid.mp,
        )

    def own(self, c):
        step = self.rows // CHUNKS
        return self.src.at[pl.ds(c * step, step)]

    def start(self):
        for c in range(CHUNKS):
            for way in (1, -1):
                pl.when(self.goes_on(way))(lambda way=way, c=c: self.hop(self.own(c), way, 0, c).start())
            for dx in range(1, self.grid.inner):
                self.aside(self.own(c), 1, 0, dx, c).start()
        me = self.grid.at(0, 0)
        whole = self.dst.at[pl.ds(pl.multiple_of(me * self.rows, self.rows), self.rows)]
        kept = pltpu.make_async_copy(self.src, whole, self.local)
        kept.start()
        kept.wait()

    def take(self, way, hops, c):
        piece = self.block(way, hops, 0, c)
        lane = (way + 1) // 2
        send, recv = self.line
        dp = (self.grid.z - way) * self.grid.inner + self.grid.x
        remote(piece, piece, send.at[lane, hops, c], recv.at[lane, hops, c], dp, self.grid.mp).wait_recv()
        if hops < self.grid.outer - 1:
            pl.when(self.goes_on(way))(lambda: self.hop(piece, way, hops, c).start())
        for dx in range(1, self.grid.inner):
            self.aside(piece, way, hops, dx, c).start()

    def take_aside(self, way, hops, c):
        for dx in range(1, self.grid.inner):
            piece = self.block(way, hops, -dx, c)
            self.aside(piece, way, hops, dx, c).wait_recv()

    def settle(self, way, hops, c):
        piece = self.own(c) if hops == 0 else self.block(way, hops, 0, c)
        if hops < self.grid.outer - 1:
            pl.when(self.goes_on(way))(lambda: self.hop(piece, way, hops, c).wait_send())
        if hops or way > 0:
            for dx in range(1, self.grid.inner):
                self.aside(piece, way, hops, dx, c).wait_send()

    def each(self, act, hops):
        for c in range(CHUNKS):
            for way in (1, -1):
                pl.when(self.arrives(way, hops))(lambda way=way, c=c: act(way, hops, c))

    def line_in(self, hops):
        self.each(self.take, hops)

    def side_in(self, hops):
        if hops:
            self.each(self.take_aside, hops)
        else:
            for c in range(CHUNKS):
                self.take_aside(1, 0, c)

    def use(self, hops, dx, apply):
        x = lax.rem(self.grid.x + (dx + self.grid.inner), self.grid.inner)
        for way in (1, -1) if hops else (1,):
            z = self.grid.z - hops * way
            pl.when(self.arrives(way, hops))(lambda z=z: apply(z * self.grid.inner + x))

    def use_side(self, hops, apply):
        for dx in range(1, self.grid.inner):
            self.use(hops, -dx, apply)

    def finish(self):
        for hops in range(self.grid.outer):
            if hops:
                self.each(self.settle, hops)
            else:
                for c in range(CHUNKS):
                    for way in (1, -1):
                        self.settle(way, 0, c)


def gather_scratch(size):
    inner = inner_of(size)
    outer = size // inner
    line = pltpu.SemaphoreType.DMA((2, outer, CHUNKS))
    side = pltpu.SemaphoreType.DMA((2, outer, inner, CHUNKS))
    return [line, line, side, side]


def times_shards(attn, gathered, out, rows):
    tokens = attn.shape[0]
    tile = min(tokens, 128)
    if rows % LANES:
        return lambda device: None

    def apply(device):
        span = pl.ds(pl.multiple_of(device * rows, rows), rows)

        def body(t, carry):
            here = pl.ds(pl.multiple_of(t * tile, tile), tile)
            out[here, :] += jnp.dot(attn[here, span], gathered[span, :], preferred_element_type=F32)
            return carry

        lax.fori_loop(0, tokens // tile, body, 0)

    return apply


def times_whole(attn, gathered, out, rows):
    if rows % LANES:
        out[...] = jnp.dot(attn[...], gathered[...], preferred_element_type=F32)


def first_kernel(
    size, starts, query_in, key_in, value_in, src, stream_in, proj_in, attn, h_out, hdot,
    query, key, value, stream, proj, gathered, mine, loads, local, send_m, recv_m, *sems
):
    grid = Grid(size)
    q_rows, width = query.shape
    num_k = key.shape[0]
    ways = num_k // q_rows
    dp = lax.axis_index("dp")
    mp = grid.mp
    others = [lax.rem(mp + d, ways) for d in range(1, ways)]
    pairs = ((query_in, query), (key_in, key), (value_in, value), (stream_in, stream), (proj_in, proj))
    loading = [pltpu.make_async_copy(there, here, loads.at[i]) for i, (there, here) in enumerate(pairs)]
    for copy in loading:
        copy.start()
    greet(grid.peers() + [(dp, other) for other in others])
    gather = Gather(grid, src, gathered, local.at[0], *sems)
    gather.start()
    for copy in loading[:3]:
        copy.wait()

    q_pos = mp * q_rows + lax.broadcasted_iota(jnp.int32, (q_rows, num_k), 0)
    k_pos = lax.broadcasted_iota(jnp.int32, (q_rows, num_k), 1)
    q_file = jnp.zeros((q_rows, num_k), jnp.int32)
    k_file = jnp.zeros((q_rows, num_k), jnp.int32)
    for f in range(starts.shape[1]):
        q_file = q_file + (starts[0, f] <= q_pos).astype(jnp.int32)
        k_file = k_file + (starts[0, f] <= k_pos).astype(jnp.int32)
    allowed = (q_file == k_file) & (k_pos <= q_pos) & (q_pos - k_pos < WINDOW)
    for h in range(HQ):
        g = h // (HQ // HK)
        scores = lax.dot_general(
            query[:, h * HD : (h + 1) * HD],
            key[:, g * HD : (g + 1) * HD],
            (((1,), (1,)), ((), ())),
            preferred_element_type=F32,
        ) * (1.0 / HD**0.5)
        scores = 50.0 * jnp.tanh(scores / 50.0)
        expo = jnp.where(allowed, jnp.exp(scores), 0.0)
        weights = (expo / jnp.sum(expo, -1, keepdims=True)).astype(BF16)
        out = jnp.dot(weights, value[:, g * HD : (g + 1) * HD], preferred_element_type=F32)
        mine[:, h * HD : (h + 1) * HD] = out.astype(BF16)
        if h == HQ - 3 and grid.outer > 1:
            gather.line_in(1)

    def rows_of(device):
        return attn.at[pl.ds(pl.multiple_of(device * q_rows, q_rows), q_rows)]

    sent = [
        remote(mine, rows_of(mp), send_m.at[d], recv_m.at[d], dp, other) for d, other in enumerate(others)
    ]
    for copy in sent:
        copy.start()
    own = pltpu.make_async_copy(mine, rows_of(mp), local.at[1])
    own.start()
    hdot[...] = jnp.zeros_like(hdot)
    for hops in range(2, grid.outer):
        gather.line_in(hops)
    own.wait()
    for d, other in enumerate(others):
        place = rows_of(lax.rem(mp + (ways - 1 - d), ways))
        remote(place, place, send_m.at[d], recv_m.at[d], dp, other).wait_recv()
    for copy in loading[3:]:
        copy.wait()
    tile = min(num_k, 128)

    def body(t, carry):
        here = pl.ds(pl.multiple_of(t * tile, tile), tile)
        h_out[here, :] = stream[here, :].astype(F32) + jnp.dot(
            attn[here, :], proj[...], preferred_element_type=F32
        )
        return carry

    lax.fori_loop(0, num_k // tile, body, 0)
    apply = times_shards(attn, gathered, hdot, src.shape[0])
    for hops in range(grid.outer):
        gather.use(hops, 0, apply)
    for hops in range(grid.outer):
        gather.side_in(hops)
        gather.use_side(hops, apply)
    times_whole(attn, gathered, hdot, src.shape[0])
    gather.finish()
    for copy in sent:
        copy.wait_send()


def first(size, ways, starts, query, key, value, src, stream, proj):
    rows, cols = src.shape
    tokens = key.shape[0]
    vmem = pl.BlockSpec(memory_space=pltpu.VMEM)
    place = pl.BlockSpec(memory_space=pl.ANY)
    loaded = (query, key, value, stream, proj)
    return pl.pallas_call(
        functools.partial(first_kernel, size),
        out_shape=(
            jax.ShapeDtypeStruct((tokens, query.shape[1]), BF16),
            jax.ShapeDtypeStruct((tokens, cols), F32),
            jax.ShapeDtypeStruct((tokens, cols), F32),
        ),
        in_specs=[pl.BlockSpec(memory_space=pltpu.SMEM), place, place, place, vmem, place, place],
        out_specs=(vmem, vmem, vmem),
        scratch_shapes=[pltpu.VMEM(array.shape, BF16) for array in loaded]
        + [
            pltpu.VMEM((rows * size, cols), BF16),
            pltpu.VMEM(query.shape, BF16),
            pltpu.SemaphoreType.DMA((len(loaded),)),
            pltpu.SemaphoreType.DMA((2,)),
            pltpu.SemaphoreType.DMA((ways,)),
            pltpu.SemaphoreType.DMA((ways,)),
        ]
        + gather_scratch(size),
        compiler_params=pltpu.CompilerParams(
            collective_id=0, has_side_effects=True, vmem_limit_bytes=VMEM_LIMIT
        ),
        name="attend_and_gather",
    )(starts, query, key, value, src, stream, proj)


def curve_kernel(ways, early, *refs):
    if early:
        part, tags, packed, z_out, r_out, extra_out, got, mine, s1, r1, s2, r2 = refs
    else:
        part, tags, z_in, r_in, packed, extra_out, got, mine, s1, r1, s2, r2 = refs
    rows = part.shape[0] // ways
    dp = lax.axis_index("dp")
    mp = lax.axis_index("mp")
    others = [lax.rem(mp + d, ways) for d in range(1, ways)]
    greet([(dp, other) for other in others])

    def rows_of(device):
        return pl.ds(pl.multiple_of(device * rows, rows), rows)

    sent = [
        remote(part.at[rows_of(other)], got.at[d], s1.at[d], r1.at[d], dp, other)
        for d, other in enumerate(others)
    ]
    for copy in sent:
        copy.start()
    total = part[rows_of(mp), :].astype(F32)
    for d, copy in enumerate(sent):
        copy.wait_recv()
        total = total + got[d].astype(F32)
    if early:
        zval = total[:, :TAGS]
        zdot = total[:, TAGS : 2 * TAGS]
        extra = total[:, 2 * TAGS :]
        sumsq = extra[:, 2:3] + extra[:, 3:4]
        rscale = lax.rsqrt(sumsq / D + NORM_EPS)
        z_out[...] = zval
        r_out[...] = jnp.broadcast_to(rscale, r_out.shape)
    else:
        zdot = total[:, :TAGS]
        extra = total[:, TAGS:]
        zval = z_in[...]
        rscale = r_in[:, 0:1]
    along = extra[:, 0:1] + extra[:, 1:2]
    extra_out[...] = extra[:8, :]
    tanh_val = jnp.tanh(rscale * zval / 30.0)
    slope = 1.0 - tanh_val * tanh_val
    expo = jnp.exp(30.0 * tanh_val)
    probs = expo / jnp.sum(expo, -1, keepdims=True)
    lane = lax.broadcasted_iota(jnp.int32, zval.shape, 1)
    onehot = (tags[rows_of(mp), :] == lane).astype(F32)
    dlogit = probs - onehot
    wgrad = dlogit * slope
    rho = jnp.sum(wgrad * zval, -1, keepdims=True)
    cube = rscale * rscale * rscale / D
    rdot = -cube * along
    mdot = rdot * zval + rscale * zdot
    ldot = slope * mdot
    pdot = probs * (ldot - jnp.sum(probs * ldot, -1, keepdims=True))
    wdot = pdot * slope - dlogit * 2.0 * tanh_val * slope * mdot / 30.0
    rhodot = jnp.sum(wdot * zval + wgrad * zdot, -1, keepdims=True)
    mixed = rdot * wgrad + rscale * wdot
    coeff = rhodot * cube + 3.0 * rho * rscale * rscale * rdot / D
    pull = rho * cube
    coeff_high = coeff.astype(BF16).astype(F32)
    pull_high = pull.astype(BF16).astype(F32)
    columns = jnp.where(lane == 0, coeff_high, 0.0)
    columns = jnp.where(lane == 1, coeff - coeff_high, columns)
    columns = jnp.where(lane == 2, pull_high, columns)
    columns = jnp.where(lane == 3, pull - pull_high, columns)
    mixed_high = mixed.astype(BF16)
    mine[:, :TAGS] = mixed_high
    mine[:, TAGS : 2 * TAGS] = (mixed - mixed_high.astype(F32)).astype(BF16)
    mine[:, 2 * TAGS :] = columns.astype(BF16)
    back = [
        remote(mine, packed.at[rows_of(mp)], s2.at[d], r2.at[d], dp, other)
        for d, other in enumerate(others)
    ]
    for copy in back:
        copy.start()
    packed[rows_of(mp), :] = mine[...]
    for d, other in enumerate(others):
        place = packed.at[rows_of(lax.rem(mp + (ways - 1 - d), ways))]
        remote(place, place, s2.at[d], r2.at[d], dp, other).wait_recv()
    for copy in sent + back:
        copy.wait_send()


def curve(ways, part, tags, state, collective_id):
    early = state is None
    tokens, width = part.shape
    rows = tokens // ways
    vmem = pl.BlockSpec(memory_space=pltpu.VMEM)
    operands = (part, tags) if early else (part, tags) + state
    out_shape = [jax.ShapeDtypeStruct((tokens, 3 * TAGS), BF16)]
    if early:
        out_shape += [jax.ShapeDtypeStruct((rows, TAGS), F32)] * 2
    out_shape += [jax.ShapeDtypeStruct((8, TAGS), F32)]
    sems = pltpu.SemaphoreType.DMA((ways,))
    return pl.pallas_call(
        functools.partial(curve_kernel, ways, early),
        out_shape=tuple(out_shape),
        in_specs=[vmem] * len(operands),
        out_specs=(vmem,) * len(out_shape),
        scratch_shapes=[
            pltpu.VMEM((ways - 1, rows, width), BF16),
            pltpu.VMEM((rows, 3 * TAGS), BF16),
            sems,
            sems,
            sems,
            sems,
        ],
        compiler_params=pltpu.CompilerParams(
            collective_id=collective_id, has_side_effects=True, vmem_limit_bytes=VMEM_LIMIT
        ),
        name="curve_early" if early else "curve_late",
    )(*operands)


def reduce_rows(grid, attn, gdot, own, full, away, kept, from_x, out, from_z, s_x, r_x, s_z, r_z):
    rows, cols = own.shape
    step = rows // STEPS
    outer, inner = grid.outer, grid.inner
    sent = []
    plans = []
    for z in range(outer):
        plan = [(k, way) for k in range(outer - 1, 0, -1) for way in (1, -1) if 0 <= z + k * way < outer]
        plans.append(plan + [(0, 1)])

    def pick(values):
        out = jnp.int32(values[0])
        for z in range(1, outer):
            out = jnp.where(grid.z == z, jnp.int32(values[z]), out)
        return out

    dists = [pick([plan[j][0] for plan in plans]) for j in range(outer)]
    ways = [pick([plan[j][1] for plan in plans]) for j in range(outer)]

    def piece(ref, c):
        return ref.at[pl.ds(c * step, step)]

    def columns_times(span):
        return lax.dot_general(
            attn[:, span], gdot[...], (((0,), (0,)), ((), ())), preferred_element_type=F32
        )

    if rows % LANES:
        for start in range(0, full.shape[0], LANES):
            full[start : start + LANES, :] = columns_times(pl.ds(start, LANES))

    def product(j, dx):
        z = grid.z + dists[j] * ways[j]
        device = z * inner + lax.rem(grid.x + dx, inner)
        span = pl.ds(pl.multiple_of(device * rows, rows), rows)
        return full[span, :] if rows % LANES else columns_times(span)

    def produce(j):
        for dx in range(1, inner):
            away[j, dx - 1] = product(j, dx).astype(BF16)

    def keep(j):
        kept[j] = product(j, 0)

    def over(j, dx, c):
        return remote(
            piece(away.at[j, dx - 1], c),
            piece(from_x.at[j, dx - 1], c),
            s_x.at[j, dx, c],
            r_x.at[j, dx, c],
            grid.at(0, dx),
            grid.mp,
        )

    def feed(j, c):
        for dx in range(1, inner):
            copy = over(j, dx, c)
            copy.start()
            sent.append(copy)

    produce(0)
    for c in range(STEPS):
        feed(0, c)
    keep(0)
    for j in range(outer):
        last = j == outer - 1
        if not last:
            produce(j + 1)
        k, way = dists[j], ways[j]
        lane = (way + 1) // 2
        behind = grid.z - way
        follows = (behind >= 0) & (behind < outer)
        ahead = (grid.z + way) * inner + grid.x
        for c in range(STEPS):
            total = piece(kept.at[j], c)[...]
            for dx in range(1, inner):
                over(j, dx, c).wait_recv()
                total = total + piece(from_x.at[j, dx - 1], c)[...].astype(F32)
            if not last:
                feed(j + 1, c)
            if not last:
                place = piece(out.at[j], c)
                came = piece(from_z.at[lane, k], c)

                @pl.when(follows)
                def _():
                    remote(came, came, s_z.at[j, c], r_z.at[lane, k, c], ahead, grid.mp).wait_recv()
                    place[...] = (total + came[...].astype(F32)).astype(BF16)

                @pl.when(jnp.logical_not(follows))
                def _():
                    place[...] = total.astype(BF16)

                copy = remote(
                    place, piece(from_z.at[lane, k - 1], c), s_z.at[j, c], r_z.at[lane, k - 1, c], ahead, grid.mp
                )
                copy.start()
                sent.append(copy)
            else:
                piece(own, c)[...] = total
        if not last:
            keep(j + 1)
    for c in range(STEPS):
        for lane in range(2):
            side = grid.z + (1 - 2 * lane)
            came = piece(from_z.at[lane, 0], c)

            @pl.when((side >= 0) & (side < outer))
            def _():
                remote(
                    came, came, s_z.at[0, c], r_z.at[lane, 0, c], side * inner + grid.x, grid.mp
                ).wait_recv()
                piece(own, c)[...] += came[...].astype(F32)
    return sent


def reduce_scratch(size, rows, cols):
    inner = inner_of(size)
    outer = size // inner
    return [
        pltpu.VMEM((size * rows, cols) if rows % LANES else (8, LANES), F32),
        pltpu.VMEM((outer, inner - 1, rows, cols), BF16),
        pltpu.VMEM((outer, rows, cols), F32),
        pltpu.VMEM((outer, inner - 1, rows, cols), BF16),
        pltpu.VMEM((outer - 1, rows, cols), BF16),
        pltpu.VMEM((2, outer, rows, cols), BF16),
        pltpu.SemaphoreType.DMA((outer, inner, STEPS)),
        pltpu.SemaphoreType.DMA((outer, inner, STEPS)),
        pltpu.SemaphoreType.DMA((outer, STEPS)),
        pltpu.SemaphoreType.DMA((2, outer, STEPS)),
    ]


REDUCE_REFS = 10


def sum_gather_kernel(size, attn, gdot, own, hdot, gathered, mine, local, *refs):
    grid = Grid(size)
    greet(grid.peers())
    sent = reduce_rows(grid, attn, gdot, own, *refs[:REDUCE_REFS])
    mine[...] = own[...].astype(BF16)
    gather = Gather(grid, mine, gathered, local.at[0], *refs[REDUCE_REFS:])
    gather.start()
    hdot[...] = jnp.zeros_like(hdot)
    apply = times_shards(attn, gathered, hdot, own.shape[0])
    gather.use(0, 0, apply)
    for hops in range(1, grid.outer):
        gather.line_in(hops)
        gather.use(hops, 0, apply)
        gather.side_in(hops - 1)
        gather.use_side(hops - 1, apply)
    gather.side_in(grid.outer - 1)
    gather.use_side(grid.outer - 1, apply)
    times_whole(attn, gathered, hdot, own.shape[0])
    gather.finish()
    for copy in sent:
        copy.wait_send()


def sum_gather(size, attn, gdot):
    tokens, total = attn.shape
    cols = gdot.shape[1]
    rows = total // size
    vmem = pl.BlockSpec(memory_space=pltpu.VMEM)
    return pl.pallas_call(
        functools.partial(sum_gather_kernel, size),
        out_shape=(
            jax.ShapeDtypeStruct((rows, cols), F32),
            jax.ShapeDtypeStruct((tokens, cols), F32),
        ),
        in_specs=[vmem, vmem],
        out_specs=(vmem, vmem),
        scratch_shapes=[
            pltpu.VMEM((total, cols), BF16),
            pltpu.VMEM((rows, cols), BF16),
            pltpu.SemaphoreType.DMA((1,)),
        ]
        + reduce_scratch(size, rows, cols)
        + gather_scratch(size),
        compiler_params=pltpu.CompilerParams(
            collective_id=2, has_side_effects=True, vmem_limit_bytes=VMEM_LIMIT
        ),
        name="sum_and_gather",
    )(attn, gdot)


def sum_kernel(size, attn, gdot, scalars, own, scalar_sum, got, s2, r2, *refs):
    grid = Grid(size)
    others = [lax.rem(lax.axis_index("dp") + d, size) for d in range(1, size)]
    greet([(other, grid.mp) for other in others])
    small = [
        remote(scalars, got.at[d], s2.at[d], r2.at[d], other, grid.mp) for d, other in enumerate(others)
    ]
    for copy in small:
        copy.start()
    sent = reduce_rows(grid, attn, gdot, own, *refs)
    total = scalars[...]
    for d, copy in enumerate(small):
        copy.wait_recv()
        total = total + got[d]
    scalar_sum[...] = total
    for copy in sent + small:
        copy.wait_send()


def sum_only(size, attn, gdot, scalars):
    cols = gdot.shape[1]
    rows = attn.shape[1] // size
    vmem = pl.BlockSpec(memory_space=pltpu.VMEM)
    return pl.pallas_call(
        functools.partial(sum_kernel, size),
        out_shape=(
            jax.ShapeDtypeStruct((rows, cols), F32),
            jax.ShapeDtypeStruct(scalars.shape, F32),
        ),
        in_specs=[vmem, vmem, vmem],
        out_specs=(vmem, vmem),
        scratch_shapes=[
            pltpu.VMEM((size - 1,) + scalars.shape, F32),
            pltpu.SemaphoreType.DMA((size - 1,)),
            pltpu.SemaphoreType.DMA((size - 1,)),
        ]
        + reduce_scratch(size, rows, cols),
        compiler_params=pltpu.CompilerParams(
            collective_id=4, has_side_effects=True, vmem_limit_bytes=VMEM_LIMIT
        ),
        name="sum_rows",
    )(attn, gdot, scalars)


def split_columns(values, tokens):
    out = []
    for value in values:
        value = jnp.broadcast_to(value, (tokens,))
        high = lax.reduce_precision(value, 8, 7)
        out += [high, value - high]
    block = jnp.stack(out, -1).astype(BF16)
    return jnp.pad(block, ((0, 0), (0, TAGS - len(out))))


def local(size, ways, queries, keys, values, stream, out_proj, norm_gain, tag_proj, direction, starts, tags):
    count = HQ * HD * D
    tokens = keys.shape[1]
    tag_column = tags[0][:, None]
    attn, h_loc, hdot = first(
        size, ways, starts, queries[0], keys[0], values[0], direction.astype(BF16), stream[0], out_proj
    )
    tag_twice = jnp.concatenate([tag_proj, tag_proj], 1)

    def scores(value):
        value = value * norm_gain
        high = lax.reduce_precision(value, 8, 7)
        low = (value - high).astype(BF16)
        return (
            jnp.dot(high.astype(BF16), tag_proj, preferred_element_type=F32)
            + jnp.dot(low, tag_proj, preferred_element_type=F32)
        ).astype(BF16)

    def tangent(packed, hdot):
        columns = packed[:, 2 * TAGS : 2 * TAGS + 4].astype(F32)
        coeff = columns[:, 0:1] + columns[:, 1:2]
        pull = columns[:, 2:3] + columns[:, 3:4]
        back = lax.dot_general(
            packed[:, : 2 * TAGS], tag_twice, (((1,), (1,)), ((), ())), preferred_element_type=F32
        )
        return (back * norm_gain - coeff * h_loc - pull * hdot).astype(BF16)

    extra = split_columns([jnp.sum(h_loc * hdot, -1), jnp.sum(h_loc * h_loc, -1)], tokens)
    part = jnp.concatenate([scores(h_loc), scores(hdot), extra], 1)
    packed, zval, rscale, _ = curve(ways, part, tag_column, None, 1)
    once, hdot = sum_gather(size, attn, tangent(packed, hdot))

    extra = split_columns(
        [jnp.sum(h_loc * hdot, -1), jnp.sum(direction * direction), jnp.sum(once * once)], tokens
    )
    part = jnp.concatenate([scores(hdot), extra], 1)
    packed, scalars = curve(ways, part, tag_column, (zval, rscale), 3)
    twice, sums = sum_only(size, attn, tangent(packed, hdot), scalars)

    early_norm = sums[0, 2] + sums[0, 3]
    product_sq = sums[0, 4] + sums[0, 5]
    sigma = 2.0 * jnp.sqrt((product_sq / count + MEAN_EPS) / (early_norm / count + MEAN_EPS))
    keep = 1.0 - DAMP
    return (
        (1.0 + keep * (1.0 + keep)) * direction
        - ((1.0 + 2.0 * keep) / sigma) * once
        + twice / sigma / sigma
    )


def solution(mesh):
    return jax.shard_map(
        functools.partial(local, mesh.shape["dp"], mesh.shape["mp"]),
        mesh=mesh,
        in_specs=(
            P("dp", "mp", None),
            P("dp", None, None),
            P("dp", None, None),
            P("dp", None, "mp"),
            P(None, "mp"),
            P("mp"),
            P("mp", None),
            P("dp", "mp"),
            P("dp", None),
            P("dp", None),
        ),
        out_specs=P("dp", "mp"),
        check_vma=False,
    )
```

```python
import functools
import types

import jax
import jax.numpy as jnp
from jax import lax
from jax.experimental import pallas as pl
from jax.experimental.pallas import tpu as pltpu
from jax.sharding import PartitionSpec as P

D = 3584
HD = 256
HQ = 8
HK = 4
TAGS = 128
WINDOW = 256

DAMP = 0.01
NORM_EPS = 1e-06
MEAN_EPS = 1e-06

MESH = pl.DeviceIdType.MESH
VMEM_LIMIT = 58 * 1024 * 1024
CHUNKS = 2
STEPS = 4
LANES = 128
F32 = jnp.float32
BF16 = jnp.bfloat16


def inner_of(size):
    return 1 << ((size.bit_length() - 1) // 2)


def remote(src, dst, send, recv, dp, mp):
    return pltpu.make_async_remote_copy(
        src_ref=src,
        dst_ref=dst,
        send_sem=send,
        recv_sem=recv,
        device_id=(dp, mp),
        device_id_type=MESH,
    )


def greet(peers):
    barrier = pltpu.get_barrier_semaphore()
    for dp, mp in peers:
        pl.semaphore_signal(barrier, inc=1, device_id=(dp, mp), device_id_type=MESH)
    pl.semaphore_wait(barrier, len(peers))


class Grid:
    def __init__(self, size):
        self.size = size
        self.inner = inner_of(size)
        self.outer = size // self.inner
        self.mp = lax.axis_index("mp")
        me = lax.axis_index("dp")
        self.z = me // self.inner
        self.x = me % self.inner

    def at(self, dz, dx):
        z = lax.rem(self.z + (dz + self.outer), self.outer)
        x = lax.rem(self.x + (dx + self.inner), self.inner)
        return z * self.inner + x

    def peers(self):
        out = [(self.at(dz, 0), self.mp) for dz in range(1, self.outer)]
        return out + [(self.at(0, dx), self.mp) for dx in range(1, self.inner)]


def part_rows(ref, device, rows, chunk):
    step = rows // CHUNKS
    return ref.at[pl.ds(pl.multiple_of(device * rows + chunk * step, step), step)]


class Gather:
    def __init__(self, grid, src, dst, local, send, recv, send_x, recv_x):
        self.grid = grid
        self.src = src
        self.dst = dst
        self.local = local
        self.line = (send, recv)
        self.side = (send_x, recv_x)
        self.rows = src.shape[0]

    def block(self, way, hops, dx, c):
        z = self.grid.z - hops * way
        x = lax.rem(self.grid.x + (dx + self.grid.inner), self.grid.inner)
        return part_rows(self.dst, z * self.grid.inner + x, self.rows, c)

    def arrives(self, way, hops):
        return self.grid.z >= hops if way > 0 else self.grid.z + hops < self.grid.outer

    def goes_on(self, way):
        return self.grid.z < self.grid.outer - 1 if way > 0 else self.grid.z > 0

    def hop(self, piece, way, hops, c):
        send, recv = self.line
        lane = (way + 1) // 2
        dp = (self.grid.z + way) * self.grid.inner + self.grid.x
        return remote(
            piece, self.block(way, hops, 0, c), send.at[lane, hops, c], recv.at[lane, hops + 1, c], dp, self.grid.mp
        )

    def aside(self, piece, way, hops, dx, c):
        send, recv = self.side
        lane = (way + 1) // 2
        return remote(
            piece,
            self.block(way, hops, 0, c),
            send.at[lane, hops, dx, c],
            recv.at[lane, hops, dx, c],
            self.grid.at(0, dx),
            self.grid.mp,
        )

    def own(self, c):
        step = self.rows // CHUNKS
        return self.src.at[pl.ds(c * step, step)]

    def start(self):
        for c in range(CHUNKS):
            for way in (1, -1):
                pl.when(self.goes_on(way))(lambda way=way, c=c: self.hop(self.own(c), way, 0, c).start())
            for dx in range(1, self.grid.inner):
                self.aside(self.own(c), 1, 0, dx, c).start()
        me = self.grid.at(0, 0)
        whole = self.dst.at[pl.ds(pl.multiple_of(me * self.rows, self.rows), self.rows)]
        kept = pltpu.make_async_copy(self.src, whole, self.local)
        kept.start()
        kept.wait()

    def take(self, way, hops, c):
        piece = self.block(way, hops, 0, c)
        lane = (way + 1) // 2
        send, recv = self.line
        dp = (self.grid.z - way) * self.grid.inner + self.grid.x
        remote(piece, piece, send.at[lane, hops, c], recv.at[lane, hops, c], dp, self.grid.mp).wait_recv()
        if hops < self.grid.outer - 1:
            pl.when(self.goes_on(way))(lambda: self.hop(piece, way, hops, c).start())
        for dx in range(1, self.grid.inner):
            self.aside(piece, way, hops, dx, c).start()

    def take_aside(self, way, hops, c):
        for dx in range(1, self.grid.inner):
            piece = self.block(way, hops, -dx, c)
            self.aside(piece, way, hops, dx, c).wait_recv()

    def settle(self, way, hops, c):
        piece = self.own(c) if hops == 0 else self.block(way, hops, 0, c)
        if hops < self.grid.outer - 1:
            pl.when(self.goes_on(way))(lambda: self.hop(piece, way, hops, c).wait_send())
        if hops or way > 0:
            for dx in range(1, self.grid.inner):
                self.aside(piece, way, hops, dx, c).wait_send()

    def each(self, act, hops):
        for c in range(CHUNKS):
            for way in (1, -1):
                pl.when(self.arrives(way, hops))(lambda way=way, c=c: act(way, hops, c))

    def line_in(self, hops):
        self.each(self.take, hops)

    def side_in(self, hops):
        if hops:
            self.each(self.take_aside, hops)
        else:
            for c in range(CHUNKS):
                self.take_aside(1, 0, c)

    def use(self, hops, dx, apply):
        x = lax.rem(self.grid.x + (dx + self.grid.inner), self.grid.inner)
        for way in (1, -1) if hops else (1,):
            z = self.grid.z - hops * way
            pl.when(self.arrives(way, hops))(lambda z=z: apply(z * self.grid.inner + x))

    def use_side(self, hops, apply):
        for dx in range(1, self.grid.inner):
            self.use(hops, -dx, apply)

    def finish(self):
        for hops in range(self.grid.outer):
            if hops:
                self.each(self.settle, hops)
            else:
                for c in range(CHUNKS):
                    for way in (1, -1):
                        self.settle(way, 0, c)


def gather_scratch(size):
    inner = inner_of(size)
    outer = size // inner
    line = pltpu.SemaphoreType.DMA((2, outer, CHUNKS))
    side = pltpu.SemaphoreType.DMA((2, outer, inner, CHUNKS))
    return [line, line, side, side]


def times_shards(attn, gathered, out, rows):
    tokens = attn.shape[0]
    tile = min(tokens, 128)
    if rows % LANES:
        return lambda device: None

    def apply(device):
        span = pl.ds(pl.multiple_of(device * rows, rows), rows)

        def body(t, carry):
            here = pl.ds(pl.multiple_of(t * tile, tile), tile)
            out[here, :] += jnp.dot(attn[here, span], gathered[span, :], preferred_element_type=F32)
            return carry

        lax.fori_loop(0, tokens // tile, body, 0)

    return apply


def times_whole(attn, gathered, out, rows):
    if rows % LANES:
        out[...] = jnp.dot(attn[...], gathered[...], preferred_element_type=F32)


def attend(ref, starts, mp, between):
    q_rows = ref.query.shape[0]
    num_k = ref.key.shape[0]
    q_pos = mp * q_rows + lax.broadcasted_iota(jnp.int32, (q_rows, num_k), 0)
    k_pos = lax.broadcasted_iota(jnp.int32, (q_rows, num_k), 1)
    q_file = jnp.zeros((q_rows, num_k), jnp.int32)
    k_file = jnp.zeros((q_rows, num_k), jnp.int32)
    for f in range(starts.shape[1]):
        q_file = q_file + (starts[0, f] <= q_pos).astype(jnp.int32)
        k_file = k_file + (starts[0, f] <= k_pos).astype(jnp.int32)
    allowed = (q_file == k_file) & (k_pos <= q_pos) & (q_pos - k_pos < WINDOW)
    for h in range(HQ):
        g = h // (HQ // HK)
        scores = lax.dot_general(
            ref.query[:, h * HD : (h + 1) * HD],
            ref.key[:, g * HD : (g + 1) * HD],
            (((1,), (1,)), ((), ())),
            preferred_element_type=F32,
        ) * (1.0 / HD**0.5)
        scores = 50.0 * jnp.tanh(scores / 50.0)
        expo = jnp.where(allowed, jnp.exp(scores), 0.0)
        weights = (expo / jnp.sum(expo, -1, keepdims=True)).astype(BF16)
        out = jnp.dot(weights, ref.value[:, g * HD : (g + 1) * HD], preferred_element_type=F32)
        ref.mine[:, h * HD : (h + 1) * HD] = out.astype(BF16)
        if h == HQ - 3:
            between()


def over_tokens(tokens, act):
    tile = min(tokens, 128)

    def body(t, carry):
        act(pl.ds(pl.multiple_of(t * tile, tile), tile), tile)
        return carry

    lax.fori_loop(0, tokens // tile, body, 0)


def high_low(value):
    high = value.astype(BF16).astype(F32)
    return [high, value - high]


def tag_scores(value, gain, tag):
    high, low = high_low(value * gain)
    out = jnp.dot(high.astype(BF16), tag, preferred_element_type=F32)
    return (out + jnp.dot(low.astype(BF16), tag, preferred_element_type=F32)).astype(BF16)


def columns_of(values, tile):
    lane = lax.broadcasted_iota(jnp.int32, (tile, TAGS), 1)
    out = jnp.zeros((tile, TAGS), F32)
    for i, value in enumerate(values):
        out = jnp.where(lane == i, value, out)
    return out.astype(BF16)


def exchange(ref, early, part, got, mine, packed, s1, r1, s2, r2):
    dp = lax.axis_index("dp")
    mp = lax.axis_index("mp")
    rows = mine.shape[0]
    ways = part.shape[0] // rows
    others = [lax.rem(mp + d, ways) for d in range(1, ways)]

    def rows_of(device):
        return pl.ds(pl.multiple_of(device * rows, rows), rows)

    sent = [
        remote(part.at[rows_of(other)], got.at[d], s1.at[d], r1.at[d], dp, other)
        for d, other in enumerate(others)
    ]
    for copy in sent:
        copy.start()
    total = part[rows_of(mp), :].astype(F32)
    for d, copy in enumerate(sent):
        copy.wait_recv()
        total = total + got[d].astype(F32)
    zdot = total[:, :TAGS]
    extra = total[:, TAGS : 2 * TAGS]
    if early:
        zval = total[:, 2 * TAGS :]
        sumsq = extra[:, 2:3] + extra[:, 3:4]
        rscale = lax.rsqrt(sumsq / D + NORM_EPS)
        ref.zval[...] = zval
        ref.rscale[...] = jnp.broadcast_to(rscale, ref.rscale.shape)
    else:
        zval = ref.zval[...]
        rscale = ref.rscale[:, 0:1]
        ref.scalars[...] = extra[:8, :]
    along = extra[:, 0:1] + extra[:, 1:2]
    tanh_val = jnp.tanh(rscale * zval / 30.0)
    slope = 1.0 - tanh_val * tanh_val
    expo = jnp.exp(30.0 * tanh_val)
    probs = expo / jnp.sum(expo, -1, keepdims=True)
    dlogit = probs - ref.onehot[rows_of(mp), :]
    wgrad = dlogit * slope
    rho = jnp.sum(wgrad * zval, -1, keepdims=True)
    cube = rscale * rscale * rscale / D
    rdot = -cube * along
    mdot = rdot * zval + rscale * zdot
    ldot = slope * mdot
    pdot = probs * (ldot - jnp.sum(probs * ldot, -1, keepdims=True))
    wdot = pdot * slope - dlogit * 2.0 * tanh_val * slope * mdot / 30.0
    rhodot = jnp.sum(wdot * zval + wgrad * zdot, -1, keepdims=True)
    mixed = rdot * wgrad + rscale * wdot
    coeff = rhodot * cube + 3.0 * rho * rscale * rscale * rdot / D
    high, low = high_low(mixed)
    mine[:, :TAGS] = high.astype(BF16)
    mine[:, TAGS : 2 * TAGS] = low.astype(BF16)
    mine[:, 2 * TAGS :] = columns_of(high_low(coeff) + high_low(rho * cube), rows)
    back = [
        remote(mine, packed.at[rows_of(mp)], s2.at[d], r2.at[d], dp, other)
        for d, other in enumerate(others)
    ]
    for copy in back:
        copy.start()
    packed[rows_of(mp), :] = mine[...]
    for d, other in enumerate(others):
        place = packed.at[rows_of(lax.rem(mp + (ways - 1 - d), ways))]
        remote(place, place, s2.at[d], r2.at[d], dp, other).wait_recv()
    for copy in sent + back:
        copy.wait_send()


def tangent(ref, packed, hdot):
    def act(here, tile):
        columns = packed[here, 2 * TAGS :].astype(F32)
        coeff = columns[:, 0:1] + columns[:, 1:2]
        pull = columns[:, 2:3] + columns[:, 3:4]
        back = jnp.zeros((tile, ref.gain.shape[1]), F32)
        for i in range(2):
            back = back + lax.dot_general(
                packed[here, i * TAGS : (i + 1) * TAGS],
                ref.tag[...],
                (((1,), (1,)), ((), ())),
                preferred_element_type=F32,
            )
        gdot = back * ref.gain[...] - coeff * ref.h[here, :] - pull * hdot[here, :]
        ref.gdot[here, :] = gdot.astype(BF16)

    over_tokens(hdot.shape[0], act)


def whole_kernel(size, names, *refs):
    ref = types.SimpleNamespace(**dict(zip(names, refs)))
    grid = Grid(size)
    dp = lax.axis_index("dp")
    mp = grid.mp
    q_rows = ref.query.shape[0]
    tokens = ref.key.shape[0]
    ways = tokens // q_rows
    rows = ref.direction.shape[0]
    others = [lax.rem(mp + d, ways) for d in range(1, ways)]
    far = [lax.rem(dp + d, size) for d in range(1, size)]
    pairs = [
        (ref.direction_in, ref.direction),
        (ref.query_in, ref.query),
        (ref.key_in, ref.key),
        (ref.value_in, ref.value),
        (ref.stream_in, ref.stream),
        (ref.proj_in, ref.proj),
    ]
    loading = [pltpu.make_async_copy(there, here, ref.loads.at[i]) for i, (there, here) in enumerate(pairs)]
    for copy in loading:
        copy.start()
    greet([(dp, other) for other in others] + [(other, mp) for other in far])
    loading[0].wait()
    ref.src[...] = ref.direction[...].astype(BF16)
    gather = Gather(grid, ref.src, ref.gathered, ref.local.at[0], *[getattr(ref, n) for n in GATHER_A])
    gather.start()
    for copy in loading[1:4]:
        copy.wait()

    def between():
        if grid.outer > 1:
            gather.line_in(1)

    attend(ref, ref.starts, mp, between)

    def rows_of(device):
        return ref.attn.at[pl.ds(pl.multiple_of(device * q_rows, q_rows), q_rows)]

    sent = [
        remote(ref.mine, rows_of(mp), ref.send_m.at[d], ref.recv_m.at[d], dp, other)
        for d, other in enumerate(others)
    ]
    for copy in sent:
        copy.start()
    own = pltpu.make_async_copy(ref.mine, rows_of(mp), ref.local.at[1])
    own.start()
    tag_ids = lax.broadcasted_iota(jnp.int32, (TAGS, tokens), 0)
    ref.onehot[...] = jnp.transpose((tag_ids == ref.tags[...]).astype(F32))
    ref.hdot[...] = jnp.zeros_like(ref.hdot)
    ref.hdot_late[...] = jnp.zeros_like(ref.hdot_late)
    early_norm = jnp.sum(ref.direction[...] * ref.direction[...], keepdims=True)
    for hops in range(2, grid.outer):
        gather.line_in(hops)
    own.wait()
    for d, other in enumerate(others):
        place = rows_of(lax.rem(mp + (ways - 1 - d), ways))
        remote(place, place, ref.send_m.at[d], ref.recv_m.at[d], dp, other).wait_recv()
    for copy in loading[4:]:
        copy.wait()

    def project(here, tile):
        h = ref.stream[here, :].astype(F32) + jnp.dot(
            ref.attn[here, :], ref.proj[...], preferred_element_type=F32
        )
        ref.h[here, :] = h
        ref.part[here, 2 * TAGS :] = tag_scores(h, ref.gain[...], ref.tag[...])

    over_tokens(tokens, project)
    apply = times_shards(ref.attn, ref.gathered, ref.hdot, rows)
    for hops in range(grid.outer):
        gather.use(hops, 0, apply)
    for hops in range(grid.outer):
        gather.side_in(hops)
        gather.use_side(hops, apply)
    times_whole(ref.attn, ref.gathered, ref.hdot, rows)

    def scores_early(here, tile):
        h = ref.h[here, :]
        hdot = ref.hdot[here, :]
        ref.part[here, :TAGS] = tag_scores(hdot, ref.gain[...], ref.tag[...])
        ref.part[here, TAGS : 2 * TAGS] = columns_of(
            high_low(jnp.sum(h * hdot, -1, keepdims=True)) + high_low(jnp.sum(h * h, -1, keepdims=True)), tile
        )

    over_tokens(tokens, scores_early)
    exchange(ref, True, ref.part, ref.got, ref.mixed, ref.packed, *[getattr(ref, n) for n in SWAP_A])
    gather.finish()
    for copy in sent:
        copy.wait_send()
    tangent(ref, ref.packed, ref.hdot)
    sent = reduce_rows(grid, ref.attn, ref.gdot, ref.once, *[getattr(ref, n) for n in REDUCE_A])
    ref.src_late[...] = ref.once[...].astype(BF16)
    gather = Gather(
        grid, ref.src_late, ref.gathered_late, ref.local.at[0], *[getattr(ref, n) for n in GATHER_B]
    )
    gather.start()
    product_sq = jnp.sum(ref.once[...] * ref.once[...], keepdims=True)
    apply = times_shards(ref.attn, ref.gathered_late, ref.hdot_late, rows)
    gather.use(0, 0, apply)
    for hops in range(1, grid.outer):
        gather.line_in(hops)
        gather.use(hops, 0, apply)
        gather.side_in(hops - 1)
        gather.use_side(hops - 1, apply)
    gather.side_in(grid.outer - 1)
    gather.use_side(grid.outer - 1, apply)
    times_whole(ref.attn, ref.gathered_late, ref.hdot_late, rows)

    def scores_late(here, tile):
        hdot = ref.hdot_late[here, :]
        ref.part_late[here, :TAGS] = tag_scores(hdot, ref.gain[...], ref.tag[...])
        ref.part_late[here, TAGS:] = columns_of(
            high_low(jnp.sum(ref.h[here, :] * hdot, -1, keepdims=True))
            + high_low(early_norm)
            + high_low(product_sq),
            tile,
        )

    over_tokens(tokens, scores_late)
    exchange(
        ref, False, ref.part_late, ref.got_late, ref.mixed_late, ref.packed_late, *[getattr(ref, n) for n in SWAP_B]
    )
    gather.finish()
    for copy in sent:
        copy.wait_send()
    small = [
        remote(ref.scalars, ref.scalars_in.at[d], ref.send_s.at[d], ref.recv_s.at[d], other, mp)
        for d, other in enumerate(far)
    ]
    for copy in small:
        copy.start()
    tangent(ref, ref.packed_late, ref.hdot_late)
    sent = reduce_rows(grid, ref.attn, ref.gdot, ref.twice, *[getattr(ref, n) for n in REDUCE_B])
    sums = ref.scalars[...]
    for d, copy in enumerate(small):
        copy.wait_recv()
        sums = sums + ref.scalars_in[d]
    count = HQ * HD * D
    norm_mean = (sums[0:1, 2:3] + sums[0:1, 3:4]) / count
    product_mean = (sums[0:1, 4:5] + sums[0:1, 5:6]) / count
    sigma = 2.0 * jnp.sqrt((product_mean + MEAN_EPS) / (norm_mean + MEAN_EPS))
    keep = 1.0 - DAMP
    ref.iterate[...] = (
        (1.0 + keep * (1.0 + keep)) * ref.direction[...]
        - ((1.0 + 2.0 * keep) / sigma) * ref.once[...]
        + ref.twice[...] / sigma / sigma
    )
    for copy in sent + small:
        copy.wait_send()


GATHER_A = ["ga0", "ga1", "ga2", "ga3"]
GATHER_B = ["gb0", "gb1", "gb2", "gb3"]
SWAP_A = ["sa0", "sa1", "sa2", "sa3"]
SWAP_B = ["sb0", "sb1", "sb2", "sb3"]
REDUCE_A = ["ra%d" % i for i in range(10)]
REDUCE_B = ["rb%d" % i for i in range(10)]


def whole(size, ways, starts, tags, gain, tag, direction, query, key, value, stream, proj):
    rows, cols = direction.shape
    tokens = key.shape[0]
    held = tokens // ways
    scratch = {
        "direction": pltpu.VMEM(direction.shape, F32),
        "query": pltpu.VMEM(query.shape, BF16),
        "key": pltpu.VMEM(key.shape, BF16),
        "value": pltpu.VMEM(value.shape, BF16),
        "stream": pltpu.VMEM(stream.shape, BF16),
        "proj": pltpu.VMEM(proj.shape, BF16),
        "src": pltpu.VMEM((rows, cols), BF16),
        "src_late": pltpu.VMEM((rows, cols), BF16),
        "gathered": pltpu.VMEM((rows * size, cols), BF16),
        "gathered_late": pltpu.VMEM((rows * size, cols), BF16),
        "mine": pltpu.VMEM(query.shape, BF16),
        "attn": pltpu.VMEM((tokens, query.shape[1]), BF16),
        "h": pltpu.VMEM((tokens, cols), F32),
        "hdot": pltpu.VMEM((tokens, cols), F32),
        "hdot_late": pltpu.VMEM((tokens, cols), F32),
        "gdot": pltpu.VMEM((tokens, cols), BF16),
        "once": pltpu.VMEM((rows, cols), F32),
        "twice": pltpu.VMEM((rows, cols), F32),
        "onehot": pltpu.VMEM((tokens, TAGS), F32),
        "zval": pltpu.VMEM((held, TAGS), F32),
        "rscale": pltpu.VMEM((held, TAGS), F32),
        "scalars": pltpu.VMEM((8, TAGS), F32),
        "scalars_in": pltpu.VMEM((size - 1, 8, TAGS), F32),
        "part": pltpu.VMEM((tokens, 3 * TAGS), BF16),
        "part_late": pltpu.VMEM((tokens, 2 * TAGS), BF16),
        "got": pltpu.VMEM((ways - 1, held, 3 * TAGS), BF16),
        "got_late": pltpu.VMEM((ways - 1, held, 2 * TAGS), BF16),
        "mixed": pltpu.VMEM((held, 3 * TAGS), BF16),
        "mixed_late": pltpu.VMEM((held, 3 * TAGS), BF16),
        "packed": pltpu.VMEM((tokens, 3 * TAGS), BF16),
        "packed_late": pltpu.VMEM((tokens, 3 * TAGS), BF16),
        "loads": pltpu.SemaphoreType.DMA((6,)),
        "local": pltpu.SemaphoreType.DMA((2,)),
        "send_m": pltpu.SemaphoreType.DMA((ways,)),
        "recv_m": pltpu.SemaphoreType.DMA((ways,)),
        "send_s": pltpu.SemaphoreType.DMA((size,)),
        "recv_s": pltpu.SemaphoreType.DMA((size,)),
    }
    for group in (SWAP_A, SWAP_B):
        scratch.update({name: pltpu.SemaphoreType.DMA((ways,)) for name in group})
    for group in (GATHER_A, GATHER_B):
        scratch.update(zip(group, gather_scratch(size)))
    for group in (REDUCE_A, REDUCE_B):
        scratch.update(zip(group, reduce_scratch(size, rows, cols)))
    names = ["starts", "tags", "gain", "tag", "direction_in", "query_in", "key_in", "value_in"]
    names += ["stream_in", "proj_in", "iterate"] + list(scratch)
    vmem = pl.BlockSpec(memory_space=pltpu.VMEM)
    place = pl.BlockSpec(memory_space=pl.ANY)
    return pl.pallas_call(
        functools.partial(whole_kernel, size, names),
        out_shape=jax.ShapeDtypeStruct((rows, cols), F32),
        in_specs=[pl.BlockSpec(memory_space=pltpu.SMEM)] + [vmem] * 3 + [place] * 6,
        out_specs=vmem,
        scratch_shapes=list(scratch.values()),
        compiler_params=pltpu.CompilerParams(
            collective_id=0, has_side_effects=True, vmem_limit_bytes=VMEM_LIMIT
        ),
        name="lissa",
    )(starts, tags, gain, tag, direction, query, key, value, stream, proj)


def reduce_rows(grid, attn, gdot, own, full, away, kept, from_x, out, from_z, s_x, r_x, s_z, r_z):
    rows, cols = own.shape
    step = rows // STEPS
    outer, inner = grid.outer, grid.inner
    sent = []
    plans = []
    for z in range(outer):
        plan = [(k, way) for k in range(outer - 1, 0, -1) for way in (1, -1) if 0 <= z + k * way < outer]
        plans.append(plan + [(0, 1)])

    def pick(values):
        out = jnp.int32(values[0])
        for z in range(1, outer):
            out = jnp.where(grid.z == z, jnp.int32(values[z]), out)
        return out

    dists = [pick([plan[j][0] for plan in plans]) for j in range(outer)]
    ways = [pick([plan[j][1] for plan in plans]) for j in range(outer)]

    def piece(ref, c):
        return ref.at[pl.ds(c * step, step)]

    def columns_times(span):
        return lax.dot_general(
            attn[:, span], gdot[...], (((0,), (0,)), ((), ())), preferred_element_type=F32
        )

    if rows % LANES:
        for start in range(0, full.shape[0], LANES):
            full[start : start + LANES, :] = columns_times(pl.ds(start, LANES))

    def product(j, dx):
        z = grid.z + dists[j] * ways[j]
        device = z * inner + lax.rem(grid.x + dx, inner)
        span = pl.ds(pl.multiple_of(device * rows, rows), rows)
        return full[span, :] if rows % LANES else columns_times(span)

    def produce(j):
        for dx in range(1, inner):
            away[j, dx - 1] = product(j, dx).astype(BF16)

    def keep(j):
        kept[j] = product(j, 0)

    def over(j, dx, c):
        return remote(
            piece(away.at[j, dx - 1], c),
            piece(from_x.at[j, dx - 1], c),
            s_x.at[j, dx, c],
            r_x.at[j, dx, c],
            grid.at(0, dx),
            grid.mp,
        )

    def feed(j, c):
        for dx in range(1, inner):
            copy = over(j, dx, c)
            copy.start()
            sent.append(copy)

    produce(0)
    for c in range(STEPS):
        feed(0, c)
    keep(0)
    for j in range(outer):
        last = j == outer - 1
        if not last:
            produce(j + 1)
        k, way = dists[j], ways[j]
        lane = (way + 1) // 2
        behind = grid.z - way
        follows = (behind >= 0) & (behind < outer)
        ahead = (grid.z + way) * inner + grid.x
        for c in range(STEPS):
            total = piece(kept.at[j], c)[...]
            for dx in range(1, inner):
                over(j, dx, c).wait_recv()
                total = total + piece(from_x.at[j, dx - 1], c)[...].astype(F32)
            if not last:
                feed(j + 1, c)
            if not last:
                place = piece(out.at[j], c)
                came = piece(from_z.at[lane, k], c)

                @pl.when(follows)
                def _():
                    remote(came, came, s_z.at[j, c], r_z.at[lane, k, c], ahead, grid.mp).wait_recv()
                    place[...] = (total + came[...].astype(F32)).astype(BF16)

                @pl.when(jnp.logical_not(follows))
                def _():
                    place[...] = total.astype(BF16)

                copy = remote(
                    place, piece(from_z.at[lane, k - 1], c), s_z.at[j, c], r_z.at[lane, k - 1, c], ahead, grid.mp
                )
                copy.start()
                sent.append(copy)
            else:
                piece(own, c)[...] = total
        if not last:
            keep(j + 1)
    for c in range(STEPS):
        for lane in range(2):
            side = grid.z + (1 - 2 * lane)
            came = piece(from_z.at[lane, 0], c)

            @pl.when((side >= 0) & (side < outer))
            def _():
                remote(
                    came, came, s_z.at[0, c], r_z.at[lane, 0, c], side * inner + grid.x, grid.mp
                ).wait_recv()
                piece(own, c)[...] += came[...].astype(F32)
    return sent


def reduce_scratch(size, rows, cols):
    inner = inner_of(size)
    outer = size // inner
    return [
        pltpu.VMEM((size * rows, cols) if rows % LANES else (8, LANES), F32),
        pltpu.VMEM((outer, inner - 1, rows, cols), BF16),
        pltpu.VMEM((outer, rows, cols), F32),
        pltpu.VMEM((outer, inner - 1, rows, cols), BF16),
        pltpu.VMEM((outer - 1, rows, cols), BF16),
        pltpu.VMEM((2, outer, rows, cols), BF16),
        pltpu.SemaphoreType.DMA((outer, inner, STEPS)),
        pltpu.SemaphoreType.DMA((outer, inner, STEPS)),
        pltpu.SemaphoreType.DMA((outer, STEPS)),
        pltpu.SemaphoreType.DMA((2, outer, STEPS)),
    ]


def local(size, ways, queries, keys, values, stream, out_proj, norm_gain, tag_proj, direction, starts, tags):
    return whole(
        size, ways, starts, tags, norm_gain[None], tag_proj, direction,
        queries[0], keys[0], values[0], stream[0], out_proj,
    )


def solution(mesh):
    return jax.shard_map(
        functools.partial(local, mesh.shape["dp"], mesh.shape["mp"]),
        mesh=mesh,
        in_specs=(
            P("dp", "mp", None),
            P("dp", None, None),
            P("dp", None, None),
            P("dp", None, "mp"),
            P(None, "mp"),
            P("mp"),
            P("mp", None),
            P("dp", "mp"),
            P("dp", None),
            P("dp", None),
        ),
        out_specs=P("dp", "mp"),
        check_vma=False,
    )
```

```python
import functools
import types

import jax
import jax.numpy as jnp
from jax import lax
from jax.experimental import pallas as pl
from jax.experimental.pallas import tpu as pltpu
from jax.sharding import PartitionSpec as P

D = 3584
HD = 256
HQ = 8
HK = 4
TAGS = 128
WINDOW = 256

DAMP = 0.01
NORM_EPS = 1e-06
MEAN_EPS = 1e-06

MESH = pl.DeviceIdType.MESH
VMEM_LIMIT = 58 * 1024 * 1024
STEPS = 4
LANES = 128
F32 = jnp.float32
BF16 = jnp.bfloat16


def inner_of(size):
    return 1 << ((size.bit_length() - 1) // 2)


def remote(src, dst, send, recv, dp, mp):
    return pltpu.make_async_remote_copy(
        src_ref=src,
        dst_ref=dst,
        send_sem=send,
        recv_sem=recv,
        device_id=(dp, mp),
        device_id_type=MESH,
    )


def greet(peers):
    barrier = pltpu.get_barrier_semaphore()
    for dp, mp in peers:
        pl.semaphore_signal(barrier, inc=1, device_id=(dp, mp), device_id_type=MESH)
    pl.semaphore_wait(barrier, len(peers))


class Grid:
    def __init__(self, size):
        self.size = size
        self.inner = inner_of(size)
        self.outer = size // self.inner
        self.mp = lax.axis_index("mp")
        me = lax.axis_index("dp")
        self.z = me // self.inner
        self.x = me % self.inner

    def at(self, dz, dx):
        z = lax.rem(self.z + (dz + self.outer), self.outer)
        x = lax.rem(self.x + (dx + self.inner), self.inner)
        return z * self.inner + x

    def peers(self):
        out = [(self.at(dz, 0), self.mp) for dz in range(1, self.outer)]
        return out + [(self.at(0, dx), self.mp) for dx in range(1, self.inner)]


def spans_of(rows):
    first = max(16, rows // 8 // 16 * 16)
    second = (rows - first) // 2 // 16 * 16
    return [(0, first), (first, second), (first + second, rows - first - second)]


class Gather:
    def __init__(self, grid, src, dst, local, send, recv, send_x, recv_x):
        self.grid = grid
        self.src = src
        self.dst = dst
        self.local = local
        self.line = (send, recv)
        self.side = (send_x, recv_x)
        self.rows = src.shape[0]
        self.spans = spans_of(self.rows)
        self.started = 0

    def block(self, way, hops, dx, c):
        z = self.grid.z - hops * way
        x = lax.rem(self.grid.x + (dx + self.grid.inner), self.grid.inner)
        start, size = self.spans[c]
        return self.dst.at[pl.ds(pl.multiple_of((z * self.grid.inner + x) * self.rows + start, 16), size)]

    def arrives(self, way, hops):
        return self.grid.z >= hops if way > 0 else self.grid.z + hops < self.grid.outer

    def goes_on(self, way):
        return self.grid.z < self.grid.outer - 1 if way > 0 else self.grid.z > 0

    def hop(self, piece, way, hops, dx, c):
        send, recv = self.line
        lane = (way + 1) // 2
        dp = (self.grid.z + way) * self.grid.inner + self.grid.x
        return remote(
            piece,
            self.block(way, hops, dx, c),
            send.at[lane, hops, dx, c],
            recv.at[lane, hops + 1, dx, c],
            dp,
            self.grid.mp,
        )

    def aside(self, piece, way, hops, dx, c):
        send, recv = self.side
        lane = (way + 1) // 2
        return remote(
            piece,
            self.block(way, hops, 0, c),
            send.at[lane, hops, dx, c],
            recv.at[lane, hops, dx, c],
            self.grid.at(0, dx),
            self.grid.mp,
        )

    def own(self, c):
        start, size = self.spans[c]
        return self.src.at[pl.ds(start, size)]

    def start(self, ready):
        while self.started < len(self.spans) and sum(self.spans[self.started]) <= ready:
            c = self.started
            for dx in range(1, self.grid.inner):
                self.aside(self.own(c), 1, 0, dx, c).start()
            for way in (1, -1):
                pl.when(self.goes_on(way))(lambda way=way, c=c: self.hop(self.own(c), way, 0, 0, c).start())
            self.started += 1

    def keep(self):
        me = self.grid.at(0, 0)
        whole = self.dst.at[pl.ds(pl.multiple_of(me * self.rows, self.rows), self.rows)]
        kept = pltpu.make_async_copy(self.src, whole, self.local)
        kept.start()
        kept.wait()

    def relay_first(self):
        for dx in range(1, self.grid.inner):
            back = self.grid.inner - dx
            piece = self.block(1, 0, back, 0)
            self.aside(piece, 1, 0, dx, 0).wait_recv()
            for way in (1, -1):
                pl.when(self.goes_on(way))(
                    lambda way=way, piece=piece, back=back: self.hop(piece, way, 0, back, 0).start()
                )

    def take(self, way, hops, c):
        lane = (way + 1) // 2
        send, recv = self.line
        dp = (self.grid.z - way) * self.grid.inner + self.grid.x
        for dx in range(1 if c else self.grid.inner):
            piece = self.block(way, hops, dx, c)
            remote(piece, piece, send.at[lane, hops, dx, c], recv.at[lane, hops, dx, c], dp, self.grid.mp).wait_recv()
            if hops < self.grid.outer - 1:
                pl.when(self.goes_on(way))(
                    lambda piece=piece, dx=dx: self.hop(piece, way, hops, dx, c).start()
                )
        if c:
            piece = self.block(way, hops, 0, c)
            for dx in range(1, self.grid.inner):
                self.aside(piece, way, hops, dx, c).start()

    def take_aside(self, way, hops, c):
        if c:
            for dx in range(1, self.grid.inner):
                piece = self.block(way, hops, -dx, c)
                self.aside(piece, way, hops, dx, c).wait_recv()

    def settle(self, way, hops, c):
        for dx in range(1 if c else self.grid.inner):
            piece = self.own(c) if hops == 0 and dx == 0 else self.block(way, hops, dx, c)
            if hops < self.grid.outer - 1:
                pl.when(self.goes_on(way))(
                    lambda piece=piece, dx=dx: self.hop(piece, way, hops, dx, c).wait_send()
                )
        if (c and hops) or (hops == 0 and way > 0):
            piece = self.block(way, hops, 0, c) if hops else self.own(c)
            for dx in range(1, self.grid.inner):
                self.aside(piece, way, hops, dx, c).wait_send()

    def each(self, act, hops):
        for c in range(len(self.spans)):
            for way in (1, -1):
                pl.when(self.arrives(way, hops))(lambda way=way, c=c: act(way, hops, c))

    def line_in(self, hops):
        self.each(self.take, hops)

    def side_in(self, hops):
        if hops:
            self.each(self.take_aside, hops)
        else:
            for c in range(len(self.spans)):
                self.take_aside(1, 0, c)

    def use(self, hops, dx, apply):
        x = lax.rem(self.grid.x + (dx + self.grid.inner), self.grid.inner)
        for way in (1, -1) if hops else (1,):
            z = self.grid.z - hops * way
            pl.when(self.arrives(way, hops))(lambda z=z: apply(z * self.grid.inner + x))

    def use_side(self, hops, apply):
        for dx in range(1, self.grid.inner):
            self.use(hops, -dx, apply)

    def finish(self):
        for hops in range(self.grid.outer):
            if hops:
                self.each(self.settle, hops)
            else:
                for c in range(len(self.spans)):
                    for way in (1, -1):
                        self.settle(way, 0, c)


def gather_scratch(size):
    inner = inner_of(size)
    sems = pltpu.SemaphoreType.DMA((2, size // inner, inner, 3))
    return [sems] * 4


def times_shards(attn, gathered, out, rows):
    tokens = attn.shape[0]
    tile = min(tokens, 128)
    if rows % LANES:
        return lambda device: None

    def apply(device):
        span = pl.ds(pl.multiple_of(device * rows, rows), rows)

        def body(t, carry):
            here = pl.ds(pl.multiple_of(t * tile, tile), tile)
            out[here, :] += jnp.dot(attn[here, span], gathered[span, :], preferred_element_type=F32)
            return carry

        lax.fori_loop(0, tokens // tile, body, 0)

    return apply


def times_whole(attn, gathered, out, rows):
    if rows % LANES:
        out[...] = jnp.dot(attn[...], gathered[...], preferred_element_type=F32)


def attend(ref, starts, mp, between):
    q_rows = ref.query.shape[0]
    num_k = ref.key.shape[0]
    q_pos = mp * q_rows + lax.broadcasted_iota(jnp.int32, (q_rows, num_k), 0)
    k_pos = lax.broadcasted_iota(jnp.int32, (q_rows, num_k), 1)
    q_file = jnp.zeros((q_rows, num_k), jnp.int32)
    k_file = jnp.zeros((q_rows, num_k), jnp.int32)
    for f in range(starts.shape[1]):
        q_file = q_file + (starts[0, f] <= q_pos).astype(jnp.int32)
        k_file = k_file + (starts[0, f] <= k_pos).astype(jnp.int32)
    allowed = (q_file == k_file) & (k_pos <= q_pos) & (q_pos - k_pos < WINDOW)
    for h in range(HQ):
        g = h // (HQ // HK)
        scores = lax.dot_general(
            ref.query[:, h * HD : (h + 1) * HD],
            ref.key[:, g * HD : (g + 1) * HD],
            (((1,), (1,)), ((), ())),
            preferred_element_type=F32,
        ) * (1.0 / HD**0.5)
        scores = 50.0 * jnp.tanh(scores / 50.0)
        expo = jnp.where(allowed, jnp.exp(scores), 0.0)
        weights = (expo / jnp.sum(expo, -1, keepdims=True)).astype(BF16)
        out = jnp.dot(weights, ref.value[:, g * HD : (g + 1) * HD], preferred_element_type=F32)
        ref.mine[:, h * HD : (h + 1) * HD] = out.astype(BF16)
        if h == HQ - 3:
            between()


def over_tokens(tokens, act):
    tile = min(tokens, 128)

    def body(t, carry):
        act(pl.ds(pl.multiple_of(t * tile, tile), tile), tile)
        return carry

    lax.fori_loop(0, tokens // tile, body, 0)


def high_low(value):
    high = value.astype(BF16).astype(F32)
    return [high, value - high]


def tag_scores(value, gain, tag):
    high, low = high_low(value * gain)
    out = jnp.dot(high.astype(BF16), tag, preferred_element_type=F32)
    return (out + jnp.dot(low.astype(BF16), tag, preferred_element_type=F32)).astype(BF16)


def columns_of(values, tile):
    lane = lax.broadcasted_iota(jnp.int32, (tile, TAGS), 1)
    out = jnp.zeros((tile, TAGS), F32)
    for i, value in enumerate(values):
        out = jnp.where(lane == i, value, out)
    return out.astype(BF16)


def exchange(ref, early, part, got, mine, packed, s1, r1, s2, r2):
    dp = lax.axis_index("dp")
    mp = lax.axis_index("mp")
    rows = mine.shape[0]
    ways = part.shape[0] // rows
    others = [lax.rem(mp + d, ways) for d in range(1, ways)]

    def rows_of(device):
        return pl.ds(pl.multiple_of(device * rows, rows), rows)

    sent = [
        remote(part.at[rows_of(other)], got.at[d], s1.at[d], r1.at[d], dp, other)
        for d, other in enumerate(others)
    ]
    for copy in sent:
        copy.start()
    total = part[rows_of(mp), :].astype(F32)
    for d, copy in enumerate(sent):
        copy.wait_recv()
        total = total + got[d].astype(F32)
    zdot = total[:, :TAGS]
    extra = total[:, TAGS : 2 * TAGS]
    if early:
        zval = total[:, 2 * TAGS :]
        sumsq = extra[:, 2:3] + extra[:, 3:4]
        rscale = lax.rsqrt(sumsq / D + NORM_EPS)
        ref.zval[...] = zval
        ref.rscale[...] = jnp.broadcast_to(rscale, ref.rscale.shape)
    else:
        zval = ref.zval[...]
        rscale = ref.rscale[:, 0:1]
        ref.scalars[...] = extra[:8, :]
    along = extra[:, 0:1] + extra[:, 1:2]
    tanh_val = jnp.tanh(rscale * zval / 30.0)
    slope = 1.0 - tanh_val * tanh_val
    expo = jnp.exp(30.0 * tanh_val)
    probs = expo / jnp.sum(expo, -1, keepdims=True)
    dlogit = probs - ref.onehot[rows_of(mp), :]
    wgrad = dlogit * slope
    rho = jnp.sum(wgrad * zval, -1, keepdims=True)
    cube = rscale * rscale * rscale / D
    rdot = -cube * along
    mdot = rdot * zval + rscale * zdot
    ldot = slope * mdot
    pdot = probs * (ldot - jnp.sum(probs * ldot, -1, keepdims=True))
    wdot = pdot * slope - dlogit * 2.0 * tanh_val * slope * mdot / 30.0
    rhodot = jnp.sum(wdot * zval + wgrad * zdot, -1, keepdims=True)
    mixed = rdot * wgrad + rscale * wdot
    coeff = rhodot * cube + 3.0 * rho * rscale * rscale * rdot / D
    high, low = high_low(mixed)
    mine[:, :TAGS] = high.astype(BF16)
    mine[:, TAGS : 2 * TAGS] = low.astype(BF16)
    mine[:, 2 * TAGS :] = columns_of(high_low(coeff) + high_low(rho * cube), rows)
    back = [
        remote(mine, packed.at[rows_of(mp)], s2.at[d], r2.at[d], dp, other)
        for d, other in enumerate(others)
    ]
    for copy in back:
        copy.start()
    packed[rows_of(mp), :] = mine[...]
    for d, other in enumerate(others):
        place = packed.at[rows_of(lax.rem(mp + (ways - 1 - d), ways))]
        remote(place, place, s2.at[d], r2.at[d], dp, other).wait_recv()
    for copy in sent + back:
        copy.wait_send()


def tangent(ref, packed, hdot):
    def act(here, tile):
        columns = packed[here, 2 * TAGS :].astype(F32)
        coeff = columns[:, 0:1] + columns[:, 1:2]
        pull = columns[:, 2:3] + columns[:, 3:4]
        back = jnp.zeros((tile, ref.gain.shape[1]), F32)
        for i in range(2):
            back = back + lax.dot_general(
                packed[here, i * TAGS : (i + 1) * TAGS],
                ref.tag[...],
                (((1,), (1,)), ((), ())),
                preferred_element_type=F32,
            )
        gdot = back * ref.gain[...] - coeff * ref.h[here, :] - pull * hdot[here, :]
        ref.gdot[here, :] = gdot.astype(BF16)

    over_tokens(hdot.shape[0], act)


def whole_kernel(size, names, *refs):
    ref = types.SimpleNamespace(**dict(zip(names, refs)))
    grid = Grid(size)
    dp = lax.axis_index("dp")
    mp = grid.mp
    q_rows = ref.query.shape[0]
    tokens = ref.key.shape[0]
    ways = tokens // q_rows
    rows = ref.direction.shape[0]
    others = [lax.rem(mp + d, ways) for d in range(1, ways)]
    far = [lax.rem(dp + d, size) for d in range(1, size)]
    pairs = [
        (ref.direction_in, ref.direction),
        (ref.query_in, ref.query),
        (ref.key_in, ref.key),
        (ref.value_in, ref.value),
        (ref.stream_in, ref.stream),
        (ref.proj_in, ref.proj),
    ]
    loading = [pltpu.make_async_copy(there, here, ref.loads.at[i]) for i, (there, here) in enumerate(pairs)]
    for copy in loading:
        copy.start()
    greet([(dp, other) for other in others] + [(other, mp) for other in far])
    loading[0].wait()
    ref.src[...] = ref.direction[...].astype(BF16)
    gather = Gather(grid, ref.src, ref.gathered, ref.local.at[0], *[getattr(ref, n) for n in GATHER_A])
    gather.start(rows)
    gather.keep()
    for copy in loading[1:4]:
        copy.wait()

    def between():
        gather.relay_first()
        if grid.outer > 1:
            gather.line_in(1)

    attend(ref, ref.starts, mp, between)

    def rows_of(device):
        return ref.attn.at[pl.ds(pl.multiple_of(device * q_rows, q_rows), q_rows)]

    sent = [
        remote(ref.mine, rows_of(mp), ref.send_m.at[d], ref.recv_m.at[d], dp, other)
        for d, other in enumerate(others)
    ]
    for copy in sent:
        copy.start()
    own = pltpu.make_async_copy(ref.mine, rows_of(mp), ref.local.at[1])
    own.start()
    ref.gain[...] = ref.gain_in[...].reshape(1, ref.gain.shape[1])
    tag_ids = lax.broadcasted_iota(jnp.int32, (TAGS, tokens), 0)
    ref.onehot[...] = jnp.transpose((tag_ids == ref.tags[...]).astype(F32))
    ref.hdot[...] = jnp.zeros_like(ref.hdot)
    ref.hdot_late[...] = jnp.zeros_like(ref.hdot_late)
    early_norm = jnp.sum(ref.direction[...] * ref.direction[...], keepdims=True)
    for hops in range(2, grid.outer):
        gather.line_in(hops)
    own.wait()
    for d, other in enumerate(others):
        place = rows_of(lax.rem(mp + (ways - 1 - d), ways))
        remote(place, place, ref.send_m.at[d], ref.recv_m.at[d], dp, other).wait_recv()
    for copy in loading[4:]:
        copy.wait()

    def project(here, tile):
        h = ref.stream[here, :].astype(F32) + jnp.dot(
            ref.attn[here, :], ref.proj[...], preferred_element_type=F32
        )
        ref.h[here, :] = h
        ref.part[here, 2 * TAGS :] = tag_scores(h, ref.gain[...], ref.tag[...])

    over_tokens(tokens, project)
    apply = times_shards(ref.attn, ref.gathered, ref.hdot, rows)
    for hops in range(grid.outer):
        gather.use(hops, 0, apply)
    for hops in range(grid.outer):
        gather.side_in(hops)
        gather.use_side(hops, apply)
    times_whole(ref.attn, ref.gathered, ref.hdot, rows)

    def scores_early(here, tile):
        h = ref.h[here, :]
        hdot = ref.hdot[here, :]
        ref.part[here, :TAGS] = tag_scores(hdot, ref.gain[...], ref.tag[...])
        ref.part[here, TAGS : 2 * TAGS] = columns_of(
            high_low(jnp.sum(h * hdot, -1, keepdims=True)) + high_low(jnp.sum(h * h, -1, keepdims=True)), tile
        )

    over_tokens(tokens, scores_early)
    exchange(ref, True, ref.part, ref.got, ref.mixed, ref.packed, *[getattr(ref, n) for n in SWAP_A])
    gather.finish()
    for copy in sent:
        copy.wait_send()
    tangent(ref, ref.packed, ref.hdot)
    gather = Gather(
        grid, ref.src_late, ref.gathered_late, ref.local.at[0], *[getattr(ref, n) for n in GATHER_B]
    )

    def done(here, ready):
        ref.src_late[here, :] = ref.once[here, :].astype(BF16)
        gather.start(ready)

    sent = reduce_rows(grid, ref.attn, ref.gdot, ref.once, done, *[getattr(ref, n) for n in REDUCE_A])
    gather.keep()
    gather.relay_first()
    product_sq = jnp.sum(ref.once[...] * ref.once[...], keepdims=True)
    apply = times_shards(ref.attn, ref.gathered_late, ref.hdot_late, rows)
    gather.use(0, 0, apply)
    for hops in range(1, grid.outer):
        gather.line_in(hops)
        gather.use(hops, 0, apply)
        gather.side_in(hops - 1)
        gather.use_side(hops - 1, apply)
    gather.side_in(grid.outer - 1)
    gather.use_side(grid.outer - 1, apply)
    times_whole(ref.attn, ref.gathered_late, ref.hdot_late, rows)

    def scores_late(here, tile):
        hdot = ref.hdot_late[here, :]
        ref.part_late[here, :TAGS] = tag_scores(hdot, ref.gain[...], ref.tag[...])
        ref.part_late[here, TAGS:] = columns_of(
            high_low(jnp.sum(ref.h[here, :] * hdot, -1, keepdims=True))
            + high_low(early_norm)
            + high_low(product_sq),
            tile,
        )

    over_tokens(tokens, scores_late)
    exchange(
        ref, False, ref.part_late, ref.got_late, ref.mixed_late, ref.packed_late, *[getattr(ref, n) for n in SWAP_B]
    )
    gather.finish()
    for copy in sent:
        copy.wait_send()
    small = [
        remote(ref.scalars, ref.scalars_in.at[d], ref.send_s.at[d], ref.recv_s.at[d], other, mp)
        for d, other in enumerate(far)
    ]
    for copy in small:
        copy.start()
    tangent(ref, ref.packed_late, ref.hdot_late)
    sent = reduce_rows(grid, ref.attn, ref.gdot, ref.twice, None, *[getattr(ref, n) for n in REDUCE_B])
    sums = ref.scalars[...]
    for d, copy in enumerate(small):
        copy.wait_recv()
        sums = sums + ref.scalars_in[d]
    count = HQ * HD * D
    norm_mean = (sums[0:1, 2:3] + sums[0:1, 3:4]) / count
    product_mean = (sums[0:1, 4:5] + sums[0:1, 5:6]) / count
    sigma = 2.0 * jnp.sqrt((product_mean + MEAN_EPS) / (norm_mean + MEAN_EPS))
    keep = 1.0 - DAMP
    ref.iterate[...] = (
        ref.twice[...] / sigma / sigma - ((1.0 + 2.0 * keep) / sigma) * ref.once[...]
    )
    for copy in sent + small:
        copy.wait_send()


GATHER_A = ["ga0", "ga1", "ga2", "ga3"]
GATHER_B = ["gb0", "gb1", "gb2", "gb3"]
SWAP_A = ["sa0", "sa1", "sa2", "sa3"]
SWAP_B = ["sb0", "sb1", "sb2", "sb3"]
REDUCE_A = ["ra%d" % i for i in range(10)]
REDUCE_B = ["rb%d" % i for i in range(10)]


def whole(size, ways, starts, tags, gain, tag, direction, query, key, value, stream, proj):
    rows, cols = direction.shape
    tokens = key.shape[0]
    held = tokens // ways
    scratch = {
        "gain": pltpu.VMEM((1, cols), F32),
        "direction": pltpu.VMEM(direction.shape, F32),
        "query": pltpu.VMEM(query.shape, BF16),
        "key": pltpu.VMEM(key.shape, BF16),
        "value": pltpu.VMEM(value.shape, BF16),
        "stream": pltpu.VMEM(stream.shape, BF16),
        "proj": pltpu.VMEM(proj.shape, BF16),
        "src": pltpu.VMEM((rows, cols), BF16),
        "src_late": pltpu.VMEM((rows, cols), BF16),
        "gathered": pltpu.VMEM((rows * size, cols), BF16),
        "gathered_late": pltpu.VMEM((rows * size, cols), BF16),
        "mine": pltpu.VMEM(query.shape, BF16),
        "attn": pltpu.VMEM((tokens, query.shape[1]), BF16),
        "h": pltpu.VMEM((tokens, cols), F32),
        "hdot": pltpu.VMEM((tokens, cols), F32),
        "hdot_late": pltpu.VMEM((tokens, cols), F32),
        "gdot": pltpu.VMEM((tokens, cols), BF16),
        "once": pltpu.VMEM((rows, cols), F32),
        "twice": pltpu.VMEM((rows, cols), F32),
        "onehot": pltpu.VMEM((tokens, TAGS), F32),
        "zval": pltpu.VMEM((held, TAGS), F32),
        "rscale": pltpu.VMEM((held, TAGS), F32),
        "scalars": pltpu.VMEM((8, TAGS), F32),
        "scalars_in": pltpu.VMEM((size - 1, 8, TAGS), F32),
        "part": pltpu.VMEM((tokens, 3 * TAGS), BF16),
        "part_late": pltpu.VMEM((tokens, 2 * TAGS), BF16),
        "got": pltpu.VMEM((ways - 1, held, 3 * TAGS), BF16),
        "got_late": pltpu.VMEM((ways - 1, held, 2 * TAGS), BF16),
        "mixed": pltpu.VMEM((held, 3 * TAGS), BF16),
        "mixed_late": pltpu.VMEM((held, 3 * TAGS), BF16),
        "packed": pltpu.VMEM((tokens, 3 * TAGS), BF16),
        "packed_late": pltpu.VMEM((tokens, 3 * TAGS), BF16),
        "loads": pltpu.SemaphoreType.DMA((6,)),
        "local": pltpu.SemaphoreType.DMA((2,)),
        "send_m": pltpu.SemaphoreType.DMA((ways,)),
        "recv_m": pltpu.SemaphoreType.DMA((ways,)),
        "send_s": pltpu.SemaphoreType.DMA((size,)),
        "recv_s": pltpu.SemaphoreType.DMA((size,)),
    }
    for group in (SWAP_A, SWAP_B):
        scratch.update({name: pltpu.SemaphoreType.DMA((ways,)) for name in group})
    for group in (GATHER_A, GATHER_B):
        scratch.update(zip(group, gather_scratch(size)))
    for group in (REDUCE_A, REDUCE_B):
        scratch.update(zip(group, reduce_scratch(size, rows, cols)))
    names = ["starts", "tags", "gain_in", "tag", "direction_in", "query_in", "key_in", "value_in"]
    names += ["stream_in", "proj_in", "iterate"] + list(scratch)
    vmem = pl.BlockSpec(memory_space=pltpu.VMEM)
    place = pl.BlockSpec(memory_space=pl.ANY)
    return pl.pallas_call(
        functools.partial(whole_kernel, size, names),
        out_shape=jax.ShapeDtypeStruct((rows, cols), F32),
        in_specs=[pl.BlockSpec(memory_space=pltpu.SMEM)] + [vmem] * 3 + [place] * 6,
        out_specs=vmem,
        scratch_shapes=list(scratch.values()),
        compiler_params=pltpu.CompilerParams(
            collective_id=0, has_side_effects=True, vmem_limit_bytes=VMEM_LIMIT
        ),
        name="lissa",
    )(starts, tags, gain, tag, direction, query, key, value, stream, proj)


def reduce_rows(grid, attn, gdot, own, done, full, away, kept, from_x, out, from_z, s_x, r_x, s_z, r_z):
    rows, cols = own.shape
    step = rows // STEPS
    outer, inner = grid.outer, grid.inner
    sent = []
    plans = []
    for z in range(outer):
        plan = [(k, way) for k in range(outer - 1, 0, -1) for way in (1, -1) if 0 <= z + k * way < outer]
        plans.append(plan + [(0, 1)])

    def pick(values):
        out = jnp.int32(values[0])
        for z in range(1, outer):
            out = jnp.where(grid.z == z, jnp.int32(values[z]), out)
        return out

    dists = [pick([plan[j][0] for plan in plans]) for j in range(outer)]
    ways = [pick([plan[j][1] for plan in plans]) for j in range(outer)]

    def piece(ref, c):
        return ref.at[pl.ds(c * step, step)]

    def columns_times(span):
        return lax.dot_general(
            attn[:, span], gdot[...], (((0,), (0,)), ((), ())), preferred_element_type=F32
        )

    if rows % LANES:
        for start in range(0, full.shape[0], LANES):
            full[start : start + LANES, :] = columns_times(pl.ds(start, LANES))

    def product(j, dx):
        z = grid.z + dists[j] * ways[j]
        device = z * inner + lax.rem(grid.x + dx, inner)
        span = pl.ds(pl.multiple_of(device * rows, rows), rows)
        return full[span, :] if rows % LANES else columns_times(span)

    def produce(j):
        for dx in range(1, inner):
            away[j, dx - 1] = product(j, dx).astype(BF16)

    def keep(j):
        kept[j] = product(j, 0)

    def over(j, dx, c):
        return remote(
            piece(away.at[j, dx - 1], c),
            piece(from_x.at[j, dx - 1], c),
            s_x.at[j, dx, c],
            r_x.at[j, dx, c],
            grid.at(0, dx),
            grid.mp,
        )

    def feed(j, c):
        for dx in range(1, inner):
            copy = over(j, dx, c)
            copy.start()
            sent.append(copy)

    produce(0)
    for c in range(STEPS):
        feed(0, c)
    keep(0)
    for j in range(outer):
        last = j == outer - 1
        if not last:
            produce(j + 1)
        k, way = dists[j], ways[j]
        lane = (way + 1) // 2
        behind = grid.z - way
        follows = (behind >= 0) & (behind < outer)
        ahead = (grid.z + way) * inner + grid.x
        for c in range(STEPS):
            total = piece(kept.at[j], c)[...]
            for dx in range(1, inner):
                over(j, dx, c).wait_recv()
                total = total + piece(from_x.at[j, dx - 1], c)[...].astype(F32)
            if not last:
                feed(j + 1, c)
            if not last:
                place = piece(out.at[j], c)
                came = piece(from_z.at[lane, k], c)

                @pl.when(follows)
                def _():
                    remote(came, came, s_z.at[j, c], r_z.at[lane, k, c], ahead, grid.mp).wait_recv()
                    place[...] = (total + came[...].astype(F32)).astype(BF16)

                @pl.when(jnp.logical_not(follows))
                def _():
                    place[...] = total.astype(BF16)

                copy = remote(
                    place, piece(from_z.at[lane, k - 1], c), s_z.at[j, c], r_z.at[lane, k - 1, c], ahead, grid.mp
                )
                copy.start()
                sent.append(copy)
            else:
                piece(own, c)[...] = total
        if not last:
            keep(j + 1)
    for c in range(STEPS):
        for lane in range(2):
            side = grid.z + (1 - 2 * lane)
            came = piece(from_z.at[lane, 0], c)

            @pl.when((side >= 0) & (side < outer))
            def _():
                remote(
                    came, came, s_z.at[0, c], r_z.at[lane, 0, c], side * inner + grid.x, grid.mp
                ).wait_recv()
                piece(own, c)[...] += came[...].astype(F32)

        if done is not None:
            done(pl.ds(c * step, step), (c + 1) * step)
    return sent


def reduce_scratch(size, rows, cols):
    inner = inner_of(size)
    outer = size // inner
    return [
        pltpu.VMEM((size * rows, cols) if rows % LANES else (8, LANES), F32),
        pltpu.VMEM((outer, inner - 1, rows, cols), BF16),
        pltpu.VMEM((outer, rows, cols), F32),
        pltpu.VMEM((outer, inner - 1, rows, cols), BF16),
        pltpu.VMEM((outer - 1, rows, cols), BF16),
        pltpu.VMEM((2, outer, rows, cols), BF16),
        pltpu.SemaphoreType.DMA((outer, inner, STEPS)),
        pltpu.SemaphoreType.DMA((outer, inner, STEPS)),
        pltpu.SemaphoreType.DMA((outer, STEPS)),
        pltpu.SemaphoreType.DMA((2, outer, STEPS)),
    ]


def local(size, ways, queries, keys, values, stream, out_proj, norm_gain, tag_proj, direction, starts, tags):
    moved = whole(
        size, ways, starts, tags, norm_gain, tag_proj, direction,
        queries[0], keys[0], values[0], stream[0], out_proj,
    )
    keep = 1.0 - DAMP
    return (1.0 + keep * (1.0 + keep)) * direction + moved


def solution(mesh):
    return jax.shard_map(
        functools.partial(local, mesh.shape["dp"], mesh.shape["mp"]),
        mesh=mesh,
        in_specs=(
            P("dp", "mp", None),
            P("dp", None, None),
            P("dp", None, None),
            P("dp", None, "mp"),
            P(None, "mp"),
            P("mp"),
            P("mp", None),
            P("dp", "mp"),
            P("dp", None),
            P("dp", None),
        ),
        out_specs=P("dp", "mp"),
        check_vma=False,
    )
```

```python
import functools
import types

import jax
import jax.numpy as jnp
from jax import lax
from jax.experimental import pallas as pl
from jax.experimental.pallas import tpu as pltpu
from jax.sharding import PartitionSpec as P

D = 3584
HD = 256
HQ = 8
HK = 4
TAGS = 128
WINDOW = 256

DAMP = 0.01
NORM_EPS = 1e-06
MEAN_EPS = 1e-06

MESH = pl.DeviceIdType.MESH
VMEM_LIMIT = 58 * 1024 * 1024
CHUNKS = 2
STEPS = 4
LANES = 128
F32 = jnp.float32
BF16 = jnp.bfloat16


def inner_of(size):
    return 1 << ((size.bit_length() - 1) // 2)


def remote(src, dst, send, recv, dp, mp):
    return pltpu.make_async_remote_copy(
        src_ref=src,
        dst_ref=dst,
        send_sem=send,
        recv_sem=recv,
        device_id=(dp, mp),
        device_id_type=MESH,
    )


def greet(peers):
    barrier = pltpu.get_barrier_semaphore()
    for dp, mp in peers:
        pl.semaphore_signal(barrier, inc=1, device_id=(dp, mp), device_id_type=MESH)
    pl.semaphore_wait(barrier, len(peers))


class Grid:
    def __init__(self, size):
        self.size = size
        self.inner = inner_of(size)
        self.outer = size // self.inner
        self.mp = lax.axis_index("mp")
        me = lax.axis_index("dp")
        self.z = me // self.inner
        self.x = me % self.inner

    def at(self, dz, dx):
        z = lax.rem(self.z + (dz + self.outer), self.outer)
        x = lax.rem(self.x + (dx + self.inner), self.inner)
        return z * self.inner + x

    def peers(self):
        out = [(self.at(dz, 0), self.mp) for dz in range(1, self.outer)]
        return out + [(self.at(0, dx), self.mp) for dx in range(1, self.inner)]


def part_rows(ref, device, rows, chunk):
    step = rows // CHUNKS
    return ref.at[pl.ds(pl.multiple_of(device * rows + chunk * step, step), step)]


class Gather:
    def __init__(self, grid, src, dst, local, send, recv, send_x, recv_x):
        self.grid = grid
        self.src = src
        self.dst = dst
        self.local = local
        self.line = (send, recv)
        self.side = (send_x, recv_x)
        self.rows = src.shape[0]

    def block(self, way, hops, dx, c):
        z = self.grid.z - hops * way
        x = lax.rem(self.grid.x + (dx + self.grid.inner), self.grid.inner)
        return part_rows(self.dst, z * self.grid.inner + x, self.rows, c)

    def arrives(self, way, hops):
        return self.grid.z >= hops if way > 0 else self.grid.z + hops < self.grid.outer

    def goes_on(self, way):
        return self.grid.z < self.grid.outer - 1 if way > 0 else self.grid.z > 0

    def hop(self, piece, way, hops, c):
        send, recv = self.line
        lane = (way + 1) // 2
        dp = (self.grid.z + way) * self.grid.inner + self.grid.x
        return remote(
            piece, self.block(way, hops, 0, c), send.at[lane, hops, c], recv.at[lane, hops + 1, c], dp, self.grid.mp
        )

    def aside(self, piece, way, hops, dx, c):
        send, recv = self.side
        lane = (way + 1) // 2
        return remote(
            piece,
            self.block(way, hops, 0, c),
            send.at[lane, hops, dx, c],
            recv.at[lane, hops, dx, c],
            self.grid.at(0, dx),
            self.grid.mp,
        )

    def own(self, c):
        step = self.rows // CHUNKS
        return self.src.at[pl.ds(c * step, step)]

    def start(self):
        for c in range(CHUNKS):
            for way in (1, -1):
                pl.when(self.goes_on(way))(lambda way=way, c=c: self.hop(self.own(c), way, 0, c).start())
            for dx in range(1, self.grid.inner):
                self.aside(self.own(c), 1, 0, dx, c).start()
        me = self.grid.at(0, 0)
        whole = self.dst.at[pl.ds(pl.multiple_of(me * self.rows, self.rows), self.rows)]
        kept = pltpu.make_async_copy(self.src, whole, self.local)
        kept.start()
        kept.wait()

    def take(self, way, hops, c):
        piece = self.block(way, hops, 0, c)
        lane = (way + 1) // 2
        send, recv = self.line
        dp = (self.grid.z - way) * self.grid.inner + self.grid.x
        remote(piece, piece, send.at[lane, hops, c], recv.at[lane, hops, c], dp, self.grid.mp).wait_recv()
        if hops < self.grid.outer - 1:
            pl.when(self.goes_on(way))(lambda: self.hop(piece, way, hops, c).start())
        for dx in range(1, self.grid.inner):
            self.aside(piece, way, hops, dx, c).start()

    def take_aside(self, way, hops, c):
        for dx in range(1, self.grid.inner):
            piece = self.block(way, hops, -dx, c)
            self.aside(piece, way, hops, dx, c).wait_recv()

    def settle(self, way, hops, c):
        piece = self.own(c) if hops == 0 else self.block(way, hops, 0, c)
        if hops < self.grid.outer - 1:
            pl.when(self.goes_on(way))(lambda: self.hop(piece, way, hops, c).wait_send())
        if hops or way > 0:
            for dx in range(1, self.grid.inner):
                self.aside(piece, way, hops, dx, c).wait_send()

    def each(self, act, hops):
        for c in range(CHUNKS):
            for way in (1, -1):
                pl.when(self.arrives(way, hops))(lambda way=way, c=c: act(way, hops, c))

    def line_in(self, hops):
        self.each(self.take, hops)

    def side_in(self, hops):
        if hops:
            self.each(self.take_aside, hops)
        else:
            for c in range(CHUNKS):
                self.take_aside(1, 0, c)

    def use(self, hops, dx, apply):
        x = lax.rem(self.grid.x + (dx + self.grid.inner), self.grid.inner)
        for way in (1, -1) if hops else (1,):
            z = self.grid.z - hops * way
            pl.when(self.arrives(way, hops))(lambda z=z: apply(z * self.grid.inner + x))

    def use_side(self, hops, apply):
        for dx in range(1, self.grid.inner):
            self.use(hops, -dx, apply)

    def finish(self):
        for hops in range(self.grid.outer):
            if hops:
                self.each(self.settle, hops)
            else:
                for c in range(CHUNKS):
                    for way in (1, -1):
                        self.settle(way, 0, c)


def gather_scratch(size):
    inner = inner_of(size)
    outer = size // inner
    line = pltpu.SemaphoreType.DMA((2, outer, CHUNKS))
    side = pltpu.SemaphoreType.DMA((2, outer, inner, CHUNKS))
    return [line, line, side, side]


def times_shards(attn, gathered, out, rows):
    tokens = attn.shape[0]
    tile = min(tokens, 128)
    if rows % LANES:
        return lambda device: None

    def apply(device):
        span = pl.ds(pl.multiple_of(device * rows, rows), rows)

        def body(t, carry):
            here = pl.ds(pl.multiple_of(t * tile, tile), tile)
            out[here, :] += jnp.dot(attn[here, span], gathered[span, :], preferred_element_type=F32)
            return carry

        lax.fori_loop(0, tokens // tile, body, 0)

    return apply


def times_whole(attn, gathered, out, rows):
    if rows % LANES:
        out[...] = jnp.dot(attn[...], gathered[...], preferred_element_type=F32)


def attend(ref, starts, mp, between):
    q_rows = ref.query.shape[0]
    num_k = ref.key.shape[0]
    q_pos = mp * q_rows + lax.broadcasted_iota(jnp.int32, (q_rows, num_k), 0)
    k_pos = lax.broadcasted_iota(jnp.int32, (q_rows, num_k), 1)
    q_file = jnp.zeros((q_rows, num_k), jnp.int32)
    k_file = jnp.zeros((q_rows, num_k), jnp.int32)
    for f in range(starts.shape[1]):
        q_file = q_file + (starts[0, f] <= q_pos).astype(jnp.int32)
        k_file = k_file + (starts[0, f] <= k_pos).astype(jnp.int32)
    allowed = (q_file == k_file) & (k_pos <= q_pos) & (q_pos - k_pos < WINDOW)
    for h in range(HQ):
        g = h // (HQ // HK)
        scores = lax.dot_general(
            ref.query[:, h * HD : (h + 1) * HD],
            ref.key[:, g * HD : (g + 1) * HD],
            (((1,), (1,)), ((), ())),
            preferred_element_type=F32,
        ) * (1.0 / HD**0.5)
        scores = 50.0 * jnp.tanh(scores / 50.0)
        expo = jnp.where(allowed, jnp.exp(scores), 0.0)
        weights = (expo / jnp.sum(expo, -1, keepdims=True)).astype(BF16)
        out = jnp.dot(weights, ref.value[:, g * HD : (g + 1) * HD], preferred_element_type=F32)
        ref.mine[:, h * HD : (h + 1) * HD] = out.astype(BF16)
        if h == HQ - 3:
            between()


def over_tokens(tokens, act):
    tile = min(tokens, 128)

    def body(t, carry):
        act(pl.ds(pl.multiple_of(t * tile, tile), tile), tile)
        return carry

    lax.fori_loop(0, tokens // tile, body, 0)


def high_low(value):
    high = value.astype(BF16).astype(F32)
    return [high, value - high]


def tag_scores(value, gain, tag):
    high, low = high_low(value * gain)
    out = jnp.dot(high.astype(BF16), tag, preferred_element_type=F32)
    return (out + jnp.dot(low.astype(BF16), tag, preferred_element_type=F32)).astype(BF16)


def columns_of(values, tile):
    lane = lax.broadcasted_iota(jnp.int32, (tile, TAGS), 1)
    out = jnp.zeros((tile, TAGS), F32)
    for i, value in enumerate(values):
        out = jnp.where(lane == i, value, out)
    return out.astype(BF16)


def exchange(ref, early, part, got, mine, packed, s1, r1, s2, r2):
    dp = lax.axis_index("dp")
    mp = lax.axis_index("mp")
    rows = mine.shape[0]
    ways = part.shape[0] // rows
    others = [lax.rem(mp + d, ways) for d in range(1, ways)]

    def rows_of(device):
        return pl.ds(pl.multiple_of(device * rows, rows), rows)

    sent = [
        remote(part.at[rows_of(other)], got.at[d], s1.at[d], r1.at[d], dp, other)
        for d, other in enumerate(others)
    ]
    for copy in sent:
        copy.start()
    total = part[rows_of(mp), :].astype(F32)
    for d, copy in enumerate(sent):
        copy.wait_recv()
        total = total + got[d].astype(F32)
    zdot = total[:, :TAGS]
    extra = total[:, TAGS : 2 * TAGS]
    if early:
        zval = total[:, 2 * TAGS :]
        sumsq = extra[:, 2:3] + extra[:, 3:4]
        rscale = lax.rsqrt(sumsq / D + NORM_EPS)
        ref.zval[...] = zval
        ref.rscale[...] = jnp.broadcast_to(rscale, ref.rscale.shape)
    else:
        zval = ref.zval[...]
        rscale = ref.rscale[:, 0:1]
        ref.scalars[...] = extra[:8, :]
    along = extra[:, 0:1] + extra[:, 1:2]
    tanh_val = jnp.tanh(rscale * zval / 30.0)
    slope = 1.0 - tanh_val * tanh_val
    expo = jnp.exp(30.0 * tanh_val)
    probs = expo / jnp.sum(expo, -1, keepdims=True)
    dlogit = probs - ref.onehot[rows_of(mp), :]
    wgrad = dlogit * slope
    rho = jnp.sum(wgrad * zval, -1, keepdims=True)
    cube = rscale * rscale * rscale / D
    rdot = -cube * along
    mdot = rdot * zval + rscale * zdot
    ldot = slope * mdot
    pdot = probs * (ldot - jnp.sum(probs * ldot, -1, keepdims=True))
    wdot = pdot * slope - dlogit * 2.0 * tanh_val * slope * mdot / 30.0
    rhodot = jnp.sum(wdot * zval + wgrad * zdot, -1, keepdims=True)
    mixed = rdot * wgrad + rscale * wdot
    coeff = rhodot * cube + 3.0 * rho * rscale * rscale * rdot / D
    high, low = high_low(mixed)
    mine[:, :TAGS] = high.astype(BF16)
    mine[:, TAGS : 2 * TAGS] = low.astype(BF16)
    mine[:, 2 * TAGS :] = columns_of(high_low(coeff) + high_low(rho * cube), rows)
    back = [
        remote(mine, packed.at[rows_of(mp)], s2.at[d], r2.at[d], dp, other)
        for d, other in enumerate(others)
    ]
    for copy in back:
        copy.start()
    packed[rows_of(mp), :] = mine[...]
    for d, other in enumerate(others):
        place = packed.at[rows_of(lax.rem(mp + (ways - 1 - d), ways))]
        remote(place, place, s2.at[d], r2.at[d], dp, other).wait_recv()
    for copy in sent + back:
        copy.wait_send()


def tangent(ref, packed, hdot):
    def act(here, tile):
        columns = packed[here, 2 * TAGS :].astype(F32)
        coeff = columns[:, 0:1] + columns[:, 1:2]
        pull = columns[:, 2:3] + columns[:, 3:4]
        back = jnp.zeros((tile, ref.gain.shape[1]), F32)
        for i in range(2):
            back = back + lax.dot_general(
                packed[here, i * TAGS : (i + 1) * TAGS],
                ref.tag[...],
                (((1,), (1,)), ((), ())),
                preferred_element_type=F32,
            )
        gdot = back * ref.gain[...] - coeff * ref.h[here, :] - pull * hdot[here, :]
        ref.gdot[here, :] = gdot.astype(BF16)

    over_tokens(hdot.shape[0], act)


def whole_kernel(size, names, *refs):
    ref = types.SimpleNamespace(**dict(zip(names, refs)))
    grid = Grid(size)
    dp = lax.axis_index("dp")
    mp = grid.mp
    q_rows = ref.query.shape[0]
    tokens = ref.key.shape[0]
    ways = tokens // q_rows
    rows = ref.direction.shape[0]
    others = [lax.rem(mp + d, ways) for d in range(1, ways)]
    far = [lax.rem(dp + d, size) for d in range(1, size)]
    pairs = [
        (ref.direction_in, ref.direction),
        (ref.query_in, ref.query),
        (ref.key_in, ref.key),
        (ref.value_in, ref.value),
        (ref.stream_in, ref.stream),
        (ref.proj_in, ref.proj),
    ]
    loading = [pltpu.make_async_copy(there, here, ref.loads.at[i]) for i, (there, here) in enumerate(pairs)]
    for copy in loading:
        copy.start()
    greet([(dp, other) for other in others] + [(other, mp) for other in far])
    loading[0].wait()
    ref.src[...] = ref.direction[...].astype(BF16)
    gather = Gather(grid, ref.src, ref.gathered, ref.local.at[0], *[getattr(ref, n) for n in GATHER_A])
    gather.start()
    for copy in loading[1:4]:
        copy.wait()

    def between():
        if grid.outer > 1:
            gather.line_in(1)

    attend(ref, ref.starts, mp, between)

    def rows_of(device):
        return ref.attn.at[pl.ds(pl.multiple_of(device * q_rows, q_rows), q_rows)]

    half = ways // 2
    sibling = mp + 1 - 2 * lax.rem(mp, 2)

    def alike(hops, core):
        return lax.rem(mp // 2 + (half - hops), half) * 2 + lax.rem(core, 2)

    sent = [remote(ref.mine, rows_of(mp), ref.send_m.at[0], ref.recv_m.at[0], dp, sibling)] + [
        remote(ref.mine, rows_of(mp), ref.send_m.at[d], ref.recv_m.at[d], dp, alike(half - d, mp))
        for d in range(1, half)
    ]
    for copy in sent:
        copy.start()
    own = pltpu.make_async_copy(ref.mine, rows_of(mp), ref.local.at[1])
    own.start()
    ref.gain[...] = ref.gain_in[...].reshape(1, ref.gain.shape[1])
    tag_ids = lax.broadcasted_iota(jnp.int32, (TAGS, tokens), 0)
    ref.onehot[...] = jnp.transpose((tag_ids == ref.tags[...]).astype(F32))
    ref.hdot[...] = jnp.zeros_like(ref.hdot)
    ref.hdot_late[...] = jnp.zeros_like(ref.hdot_late)
    early_norm = jnp.sum(ref.direction[...] * ref.direction[...], keepdims=True)
    for hops in range(2, grid.outer):
        gather.line_in(hops)
    own.wait()
    for d in range(1, half):
        place = rows_of(alike(d, mp))
        remote(place, place, ref.send_m.at[d], ref.recv_m.at[d], dp, sibling).wait_recv()
        copy = remote(place, place, ref.send_m.at[half + d], ref.recv_m.at[half + d], dp, sibling)
        copy.start()
        sent.append(copy)
    for d in range(half):
        place = rows_of(alike(d, mp + 1))
        slot = half + d if d else 0
        remote(place, place, ref.send_m.at[slot], ref.recv_m.at[slot], dp, sibling).wait_recv()
    for copy in loading[4:]:
        copy.wait()

    def project(here, tile):
        h = ref.stream[here, :].astype(F32) + jnp.dot(
            ref.attn[here, :], ref.proj[...], preferred_element_type=F32
        )
        ref.h[here, :] = h
        ref.part[here, 2 * TAGS :] = tag_scores(h, ref.gain[...], ref.tag[...])

    over_tokens(tokens, project)
    apply = times_shards(ref.attn, ref.gathered, ref.hdot, rows)
    for hops in range(grid.outer):
        gather.use(hops, 0, apply)
    for hops in range(grid.outer):
        gather.side_in(hops)
        gather.use_side(hops, apply)
    times_whole(ref.attn, ref.gathered, ref.hdot, rows)

    def scores_early(here, tile):
        h = ref.h[here, :]
        hdot = ref.hdot[here, :]
        ref.part[here, :TAGS] = tag_scores(hdot, ref.gain[...], ref.tag[...])
        ref.part[here, TAGS : 2 * TAGS] = columns_of(
            high_low(jnp.sum(h * hdot, -1, keepdims=True)) + high_low(jnp.sum(h * h, -1, keepdims=True)), tile
        )

    over_tokens(tokens, scores_early)
    exchange(ref, True, ref.part, ref.got, ref.mixed, ref.packed, *[getattr(ref, n) for n in SWAP_A])
    gather.finish()
    for copy in sent:
        copy.wait_send()
    tangent(ref, ref.packed, ref.hdot)
    sent = reduce_rows(grid, ref.attn, ref.gdot, ref.once, *[getattr(ref, n) for n in REDUCE_A])
    ref.src_late[...] = ref.once[...].astype(BF16)
    gather = Gather(
        grid, ref.src_late, ref.gathered_late, ref.local.at[0], *[getattr(ref, n) for n in GATHER_B]
    )
    gather.start()
    product_sq = jnp.sum(ref.once[...] * ref.once[...], keepdims=True)
    apply = times_shards(ref.attn, ref.gathered_late, ref.hdot_late, rows)
    gather.use(0, 0, apply)
    for hops in range(1, grid.outer):
        gather.line_in(hops)
        gather.use(hops, 0, apply)
        gather.side_in(hops - 1)
        gather.use_side(hops - 1, apply)
    gather.side_in(grid.outer - 1)
    gather.use_side(grid.outer - 1, apply)
    times_whole(ref.attn, ref.gathered_late, ref.hdot_late, rows)

    def scores_late(here, tile):
        hdot = ref.hdot_late[here, :]
        ref.part_late[here, :TAGS] = tag_scores(hdot, ref.gain[...], ref.tag[...])
        ref.part_late[here, TAGS:] = columns_of(
            high_low(jnp.sum(ref.h[here, :] * hdot, -1, keepdims=True))
            + high_low(early_norm)
            + high_low(product_sq),
            tile,
        )

    over_tokens(tokens, scores_late)
    exchange(
        ref, False, ref.part_late, ref.got_late, ref.mixed_late, ref.packed_late, *[getattr(ref, n) for n in SWAP_B]
    )
    gather.finish()
    for copy in sent:
        copy.wait_send()
    small = [
        remote(ref.scalars, ref.scalars_in.at[d], ref.send_s.at[d], ref.recv_s.at[d], other, mp)
        for d, other in enumerate(far)
    ]
    for copy in small:
        copy.start()
    tangent(ref, ref.packed_late, ref.hdot_late)
    sent = reduce_rows(grid, ref.attn, ref.gdot, ref.twice, *[getattr(ref, n) for n in REDUCE_B])
    sums = ref.scalars[...]
    for d, copy in enumerate(small):
        copy.wait_recv()
        sums = sums + ref.scalars_in[d]
    count = HQ * HD * D
    norm_mean = (sums[0:1, 2:3] + sums[0:1, 3:4]) / count
    product_mean = (sums[0:1, 4:5] + sums[0:1, 5:6]) / count
    sigma = 2.0 * jnp.sqrt((product_mean + MEAN_EPS) / (norm_mean + MEAN_EPS))
    keep = 1.0 - DAMP
    ref.iterate[...] = (
        (1.0 + keep * (1.0 + keep)) * ref.direction[...]
        - ((1.0 + 2.0 * keep) / sigma) * ref.once[...]
        + ref.twice[...] / sigma / sigma
    )
    for copy in sent + small:
        copy.wait_send()


GATHER_A = ["ga0", "ga1", "ga2", "ga3"]
GATHER_B = ["gb0", "gb1", "gb2", "gb3"]
SWAP_A = ["sa0", "sa1", "sa2", "sa3"]
SWAP_B = ["sb0", "sb1", "sb2", "sb3"]
REDUCE_A = ["ra%d" % i for i in range(10)]
REDUCE_B = ["rb%d" % i for i in range(10)]


def whole(size, ways, starts, tags, gain, tag, direction, query, key, value, stream, proj):
    rows, cols = direction.shape
    tokens = key.shape[0]
    held = tokens // ways
    scratch = {
        "gain": pltpu.VMEM((1, cols), F32),
        "direction": pltpu.VMEM(direction.shape, F32),
        "query": pltpu.VMEM(query.shape, BF16),
        "key": pltpu.VMEM(key.shape, BF16),
        "value": pltpu.VMEM(value.shape, BF16),
        "stream": pltpu.VMEM(stream.shape, BF16),
        "proj": pltpu.VMEM(proj.shape, BF16),
        "src": pltpu.VMEM((rows, cols), BF16),
        "src_late": pltpu.VMEM((rows, cols), BF16),
        "gathered": pltpu.VMEM((rows * size, cols), BF16),
        "gathered_late": pltpu.VMEM((rows * size, cols), BF16),
        "mine": pltpu.VMEM(query.shape, BF16),
        "attn": pltpu.VMEM((tokens, query.shape[1]), BF16),
        "h": pltpu.VMEM((tokens, cols), F32),
        "hdot": pltpu.VMEM((tokens, cols), F32),
        "hdot_late": pltpu.VMEM((tokens, cols), F32),
        "gdot": pltpu.VMEM((tokens, cols), BF16),
        "once": pltpu.VMEM((rows, cols), F32),
        "twice": pltpu.VMEM((rows, cols), F32),
        "onehot": pltpu.VMEM((tokens, TAGS), F32),
        "zval": pltpu.VMEM((held, TAGS), F32),
        "rscale": pltpu.VMEM((held, TAGS), F32),
        "scalars": pltpu.VMEM((8, TAGS), F32),
        "scalars_in": pltpu.VMEM((size - 1, 8, TAGS), F32),
        "part": pltpu.VMEM((tokens, 3 * TAGS), BF16),
        "part_late": pltpu.VMEM((tokens, 2 * TAGS), BF16),
        "got": pltpu.VMEM((ways - 1, held, 3 * TAGS), BF16),
        "got_late": pltpu.VMEM((ways - 1, held, 2 * TAGS), BF16),
        "mixed": pltpu.VMEM((held, 3 * TAGS), BF16),
        "mixed_late": pltpu.VMEM((held, 3 * TAGS), BF16),
        "packed": pltpu.VMEM((tokens, 3 * TAGS), BF16),
        "packed_late": pltpu.VMEM((tokens, 3 * TAGS), BF16),
        "loads": pltpu.SemaphoreType.DMA((6,)),
        "local": pltpu.SemaphoreType.DMA((2,)),
        "send_m": pltpu.SemaphoreType.DMA((ways,)),
        "recv_m": pltpu.SemaphoreType.DMA((ways,)),
        "send_s": pltpu.SemaphoreType.DMA((size,)),
        "recv_s": pltpu.SemaphoreType.DMA((size,)),
    }
    for group in (SWAP_A, SWAP_B):
        scratch.update({name: pltpu.SemaphoreType.DMA((ways,)) for name in group})
    for group in (GATHER_A, GATHER_B):
        scratch.update(zip(group, gather_scratch(size)))
    for group in (REDUCE_A, REDUCE_B):
        scratch.update(zip(group, reduce_scratch(size, rows, cols)))
    names = ["starts", "tags", "gain_in", "tag", "direction_in", "query_in", "key_in", "value_in"]
    names += ["stream_in", "proj_in", "iterate"] + list(scratch)
    vmem = pl.BlockSpec(memory_space=pltpu.VMEM)
    place = pl.BlockSpec(memory_space=pl.ANY)
    return pl.pallas_call(
        functools.partial(whole_kernel, size, names),
        out_shape=jax.ShapeDtypeStruct((rows, cols), F32),
        in_specs=[pl.BlockSpec(memory_space=pltpu.SMEM)] + [vmem] * 3 + [place] * 6,
        out_specs=vmem,
        scratch_shapes=list(scratch.values()),
        compiler_params=pltpu.CompilerParams(
            collective_id=0, has_side_effects=True, vmem_limit_bytes=VMEM_LIMIT
        ),
        name="lissa",
    )(starts, tags, gain, tag, direction, query, key, value, stream, proj)


def reduce_rows(grid, attn, gdot, own, full, away, kept, from_x, out, from_z, s_x, r_x, s_z, r_z):
    rows, cols = own.shape
    step = rows // STEPS
    outer, inner = grid.outer, grid.inner
    sent = []
    plans = []
    for z in range(outer):
        plan = [(k, way) for k in range(outer - 1, 0, -1) for way in (1, -1) if 0 <= z + k * way < outer]
        plans.append(plan + [(0, 1)])

    def pick(values):
        out = jnp.int32(values[0])
        for z in range(1, outer):
            out = jnp.where(grid.z == z, jnp.int32(values[z]), out)
        return out

    dists = [pick([plan[j][0] for plan in plans]) for j in range(outer)]
    ways = [pick([plan[j][1] for plan in plans]) for j in range(outer)]

    def piece(ref, c):
        return ref.at[pl.ds(c * step, step)]

    def columns_times(span):
        return lax.dot_general(
            attn[:, span], gdot[...], (((0,), (0,)), ((), ())), preferred_element_type=F32
        )

    if rows % LANES:
        for start in range(0, full.shape[0], LANES):
            full[start : start + LANES, :] = columns_times(pl.ds(start, LANES))

    def product(j, dx):
        z = grid.z + dists[j] * ways[j]
        device = z * inner + lax.rem(grid.x + dx, inner)
        span = pl.ds(pl.multiple_of(device * rows, rows), rows)
        return full[span, :] if rows % LANES else columns_times(span)

    def produce(j):
        for dx in range(1, inner):
            away[j, dx - 1] = product(j, dx).astype(BF16)

    def keep(j):
        kept[j] = product(j, 0)

    def over(j, dx, c):
        return remote(
            piece(away.at[j, dx - 1], c),
            piece(from_x.at[j, dx - 1], c),
            s_x.at[j, dx, c],
            r_x.at[j, dx, c],
            grid.at(0, dx),
            grid.mp,
        )

    def feed(j, c):
        for dx in range(1, inner):
            copy = over(j, dx, c)
            copy.start()
            sent.append(copy)

    produce(0)
    for c in range(STEPS):
        feed(0, c)
    keep(0)
    for j in range(outer):
        last = j == outer - 1
        if not last:
            produce(j + 1)
        k, way = dists[j], ways[j]
        lane = (way + 1) // 2
        behind = grid.z - way
        follows = (behind >= 0) & (behind < outer)
        ahead = (grid.z + way) * inner + grid.x
        for c in range(STEPS):
            total = piece(kept.at[j], c)[...]
            for dx in range(1, inner):
                over(j, dx, c).wait_recv()
                total = total + piece(from_x.at[j, dx - 1], c)[...].astype(F32)
            if not last:
                feed(j + 1, c)
            if not last:
                place = piece(out.at[j], c)
                came = piece(from_z.at[lane, k], c)

                @pl.when(follows)
                def _():
                    remote(came, came, s_z.at[j, c], r_z.at[lane, k, c], ahead, grid.mp).wait_recv()
                    place[...] = (total + came[...].astype(F32)).astype(BF16)

                @pl.when(jnp.logical_not(follows))
                def _():
                    place[...] = total.astype(BF16)

                copy = remote(
                    place, piece(from_z.at[lane, k - 1], c), s_z.at[j, c], r_z.at[lane, k - 1, c], ahead, grid.mp
                )
                copy.start()
                sent.append(copy)
            else:
                piece(own, c)[...] = total
        if not last:
            keep(j + 1)
    for c in range(STEPS):
        for lane in range(2):
            side = grid.z + (1 - 2 * lane)
            came = piece(from_z.at[lane, 0], c)

            @pl.when((side >= 0) & (side < outer))
            def _():
                remote(
                    came, came, s_z.at[0, c], r_z.at[lane, 0, c], side * inner + grid.x, grid.mp
                ).wait_recv()
                piece(own, c)[...] += came[...].astype(F32)
    return sent


def reduce_scratch(size, rows, cols):
    inner = inner_of(size)
    outer = size // inner
    return [
        pltpu.VMEM((size * rows, cols) if rows % LANES else (8, LANES), F32),
        pltpu.VMEM((outer, inner - 1, rows, cols), BF16),
        pltpu.VMEM((outer, rows, cols), F32),
        pltpu.VMEM((outer, inner - 1, rows, cols), BF16),
        pltpu.VMEM((outer - 1, rows, cols), BF16),
        pltpu.VMEM((2, outer, rows, cols), BF16),
        pltpu.SemaphoreType.DMA((outer, inner, STEPS)),
        pltpu.SemaphoreType.DMA((outer, inner, STEPS)),
        pltpu.SemaphoreType.DMA((outer, STEPS)),
        pltpu.SemaphoreType.DMA((2, outer, STEPS)),
    ]


def local(size, ways, queries, keys, values, stream, out_proj, norm_gain, tag_proj, direction, starts, tags):
    return whole(
        size, ways, starts, tags, norm_gain, tag_proj, direction,
        queries[0], keys[0], values[0], stream[0], out_proj,
    )


def solution(mesh):
    return jax.shard_map(
        functools.partial(local, mesh.shape["dp"], mesh.shape["mp"]),
        mesh=mesh,
        in_specs=(
            P("dp", "mp", None),
            P("dp", None, None),
            P("dp", None, None),
            P("dp", None, "mp"),
            P(None, "mp"),
            P("mp"),
            P("mp", None),
            P("dp", "mp"),
            P("dp", None),
            P("dp", None),
        ),
        out_specs=P("dp", "mp"),
        check_vma=False,
    )
```
